128 devices in a mesh: section: 2 (over x_hi), dp: 16 (over y, x_lo, core), tensor: 4 (over z).
Axes of the slice: x: 4 (x_hi: 2, x_lo: 2; x = x_hi * 2 + x_lo), y: 4, z: 4, core: 2. Of those that a mesh axis runs over, the one named last changes fastest.
Arguments:
- inputs: bfloat16 [2, 8192, 768], P(None, 'dp'), may hold values from -6 to 6
- cotangent: bfloat16 [2, 8192, 768], P(None, 'dp'), may hold values from -6 to 6
- seq_lengths: int32 [2, 16, 4], P(None, 'dp'), may hold values from 0 to 512, as said below
- w_qkv: bfloat16 [2, 768, 3, 768], P('section', 'dp', None, 'tensor'), may hold values from -0.21875 to 0.21875
- b_qkv: float32 [2, 3, 768], P('section', None, 'tensor'), may hold values from -1.8 to 1.8
- w_attn_out: bfloat16 [2, 768, 768], P('section', 'tensor', 'dp'), may hold values from -0.625 to 0.625
- w_in: bfloat16 [2, 768, 3072], P('section', 'dp', 'tensor'), may hold values from -0.21875 to 0.21875
- b_in: float32 [2, 3072], P('section', 'tensor'), may hold values from -1.8 to 1.8
- w_out: bfloat16 [2, 3072, 768], P('section', 'tensor', 'dp'), may hold values from -0.109375 to 0.109375
- b_out: float32 [2, 768], P('section'), may hold values from -1.8 to 1.8
- norm_gains: float32 [2, 2, 768], P('section'), may hold values from 0.5 to 1.5
- norm_biases: float32 [2, 2, 768], P('section'), may hold values from -1.8 to 1.8
Outputs:
- section_out: bfloat16 [2, 2, 8192, 768], P('section', None, 'dp', 'tensor')
- input_grads: bfloat16 [2, 2, 8192, 768], P('section', None, 'dp', 'tensor')
- grad_w_qkv: float32 [2, 768, 3, 768], P('section', 'dp', None, 'tensor')
- grad_b_qkv: float32 [2, 3, 768], P('section', None, 'tensor')
- grad_w_attn_out: float32 [2, 768, 768], P('section', 'tensor', 'dp')
- grad_w_in: float32 [2, 768, 3072], P('section', 'dp', 'tensor')
- grad_b_in: float32 [2, 3072], P('section', 'tensor')
- grad_w_out: float32 [2, 3072, 768], P('section', 'tensor', 'dp')
- grad_b_out: float32 [2, 768], P('section')
- grad_norm_gains: float32 [2, 2, 768], P('section')
- grad_norm_biases: float32 [2, 2, 768], P('section')
The draws below stay inside these ranges and needn't reach their ends.
Inputs may be any that keep to these rules, and one draw needn't show every extreme that they name: `seq_lengths`: sequence j of a slot takes ceil(length / 128) blocks, all sequences of a slot together at most 4 blocks; zero lengths (absent sequences) stand after all others; in every micro-batch one data group's slot holds a single sequence of 512 tokens.
All inputs are finite; a program needn't handle non-finite values.
Results may differ from the reference program's by a relative error of at most 0.023.
Values may be sent and summed in bfloat16 or wider, within the bound.
A program may use at most 128 MiB of HBM per device.

```python
import math
import jax
import jax.numpy as jnp
import numpy as np
from jax import lax

D = 768
HEADS = 12
HD = 64
FF = 3072
ROT = 16
BLOCK = 128
NB = 4
SEQS = 4
MB = 2
SLOT = 512
TOKENS = 8192
N_DP = 16


COMPOSITIONS = np.array([[4, 0, 0, 0], [3, 1, 0, 0], [1, 3, 0, 0], [2, 2, 0, 0], [2, 1, 1, 0], [1, 1, 1, 1], [3, 0, 0, 0], [1, 2, 0, 0], [1, 1, 1, 0], [2, 0, 0, 0], [1, 1, 0, 0], [1, 0, 0, 0]], dtype=np.int32)


def draw_seq_lengths(key, part):
    key = jax.random.fold_in(key, 7)
    pick_key, fill_key, full_key = jax.random.split(key, 3)
    patterns = jnp.asarray(COMPOSITIONS)
    picked = jax.random.randint(pick_key, (MB, N_DP), 0, patterns.shape[0])
    counts = jnp.take(patterns, picked, axis=0)
    extras = jax.random.randint(fill_key, (MB, N_DP, SEQS), 1, BLOCK + 1)
    lengths = jnp.where(counts > 0, (counts - 1) * BLOCK + extras, 0)
    chosen = jax.random.randint(full_key, (MB,), 0, N_DP)
    full_row = (jnp.arange(SEQS) == 0).astype(jnp.int32) * (NB * BLOCK)
    is_full = jnp.arange(N_DP)[None, :] == chosen[:, None]
    lengths = jnp.where(is_full[:, :, None], full_row[None, None, :], lengths)
    return lengths.astype(jnp.int32)


def shard_levels(stream_key, shape, cuts, smallest, top_value):
    loudness, own = 1.0, jax.random.fold_in(stream_key, 6)
    for dim, blocks in cuts:
        heights = jnp.exp(jax.random.uniform(jax.random.fold_in(own, dim), (blocks,), jnp.float32, smallest / len(cuts), top_value / len(cuts)))
        loudness = loudness * jnp.repeat(heights, shape[dim] // blocks).reshape([-1 if axis == dim else 1 for axis in range(len(shape))])
    return loudness


def gaussian(own_key, extent, width, most, cuts=(), kind=jnp.bfloat16):
    factor_of = shard_levels(own_key, extent, cuts, -0.22, 0.18) if cuts else 1.0
    result = jax.random.normal(own_key, extent, jnp.float32) * width * factor_of
    return jnp.minimum(jnp.maximum(result, -most), most).astype(kind)


def setup_inputs(seed: int = 0) -> dict:
    splits = jax.random.split(jax.random.key(seed), 13)
    inputs = gaussian(splits[0], (MB, TOKENS, D), 1.0, 6.0, ((1, 16),))
    cotangent = gaussian(splits[1], (MB, TOKENS, D), 1.0, 6.0, ((1, 16),))
    seq_lengths = draw_seq_lengths(jax.random.fold_in(splits[12], 71), 0)
    w_qkv = gaussian(splits[3], (2, D, 3, D), D ** -0.5, 0.21875, ((0, 2), (1, 16), (3, 4)))
    b_qkv = gaussian(splits[4], (2, 3, D), 0.3, 1.8, ((0, 2), (2, 4)), jnp.float32)
    w_attn_out = gaussian(splits[5], (2, D, D), (D // 8) ** -0.5, 0.625, ((0, 2), (1, 4), (2, 16)))
    w_in = gaussian(splits[6], (2, D, FF), D ** -0.5, 0.21875, ((0, 2), (1, 16), (2, 4)))
    b_in = gaussian(splits[7], (2, FF), 0.3, 1.8, ((0, 2), (1, 4)), jnp.float32)
    w_out = gaussian(splits[8], (2, FF, D), FF ** -0.5, 0.109375, ((0, 2), (1, 4), (2, 16)))
    b_out = gaussian(splits[9], (2, D), 0.3, 1.8, ((0, 2),), jnp.float32)
    norm_gains = jnp.clip(1.0 + 0.1 * jax.random.normal(splits[10], (2, 2, D), jnp.float32), 0.5, 1.5)
    norm_biases = gaussian(splits[11], (2, 2, D), 0.3, 1.8, ((0, 2),), jnp.float32)
    return dict(inputs=inputs, cotangent=cotangent, seq_lengths=seq_lengths, w_qkv=w_qkv, b_qkv=b_qkv, w_attn_out=w_attn_out, w_in=w_in, b_in=b_in, w_out=w_out, b_out=b_out, norm_gains=norm_gains, norm_biases=norm_biases)


EPSILON = 1e-05
MASKED = -1e+30
HIGHEST_PREC = lax.Precision.HIGHEST

@jax.custom_vjp
def low(v):
    return lax.optimization_barrier(v.astype(jnp.bfloat16)).astype(jnp.float32)

@jax.custom_vjp
def low_back(v):
    return v

def low_keep(v):
    return (low(v), None)

def low_pass(kept, grad):
    return (grad,)

def back_keep(v):
    return (v, None)

def back_low(kept, grad):
    return (low(grad),)
low.defvjp(low_keep, low_pass)
low_back.defvjp(back_keep, back_low)

def layer_norm(values, gain, shift_term):
    average = lax.optimization_barrier(jnp.mean(values, axis=-1, keepdims=True))
    centred = values - average
    spread = lax.optimization_barrier(jnp.mean(centred * centred, axis=-1, keepdims=True))
    return centred * lax.rsqrt(spread + EPSILON) * gain + shift_term

def arrange(lengths):
    blocks = (lengths + BLOCK - 1) // BLOCK
    block_ends = jnp.cumsum(blocks).astype(jnp.int32)
    places = jnp.arange(SLOT, dtype=jnp.int32)
    owners = lax.optimization_barrier(jnp.sum((block_ends[None, :] <= (places // BLOCK)[:, None]).astype(jnp.int32), axis=1))
    starts = jnp.concatenate([jnp.zeros((1,), jnp.int32), block_ends]) * BLOCK
    limits = jnp.concatenate([lengths.astype(jnp.int32), jnp.zeros((1,), jnp.int32)])
    chosen = (owners[:, None] == jnp.arange(SEQS + 1, dtype=jnp.int32)[None, :]).astype(jnp.int32)
    offset = places - lax.optimization_barrier(jnp.sum(chosen * starts[None, :], axis=1))
    seq_len = lax.optimization_barrier(jnp.sum(chosen * limits[None, :], axis=1))
    allowed = (owners[:, None] == owners[None, :]) & (offset[None, :] <= offset[:, None]) & ((offset[None, :] < seq_len[None, :]) | (places[:, None] == places[None, :]))
    half_rot = ROT // 2
    inv_freq = 1.0 / 10000.0 ** (jnp.arange(half_rot, dtype=jnp.float32) * 2.0 / ROT)
    angles = offset.astype(jnp.float32)[:, None] * inv_freq[None, :]
    return (jnp.cos(angles), jnp.sin(angles), allowed)

def rotate(values, cosines, sines):
    half_rot = ROT // 2
    cos_rows = cosines[:, None, :]
    sin_rows = sines[:, None, :]
    first = values[..., :half_rot]
    second = values[..., half_rot:ROT]
    return jnp.concatenate([first * cos_rows - second * sin_rows, second * cos_rows + first * sin_rows, values[..., ROT:]], axis=-1)

def attend(packed):
    pre_slot, lengths = packed
    cosines, sines, allowed = arrange(lengths)
    query = low(rotate(pre_slot[:, 0], cosines, sines))
    key_rot = low(rotate(pre_slot[:, 1], cosines, sines))
    value = low(pre_slot[:, 2])
    scores = jnp.einsum('qhd,khd->hqk', query, key_rot, precision=HIGHEST_PREC) * (1.0 / math.sqrt(HD))
    scores = low_back(scores)
    masked = jnp.where(allowed[None], scores, MASKED)
    top_score = lax.optimization_barrier(jnp.max(masked, axis=-1, keepdims=True))
    weights = jnp.where(allowed[None], jnp.exp(masked - top_score), 0.0)
    probs = low(weights / lax.optimization_barrier(jnp.sum(weights, axis=-1, keepdims=True)))
    return jnp.einsum('hqk,khd->qhd', probs, value, precision=HIGHEST_PREC)

def layer(acts, lengths, w_qkv, b_qkv, w_attn_out, w_in, b_in, w_out, b_out, gains, shifts):
    slots = acts.shape[0]
    normed = low(layer_norm(acts, gains[0], shifts[0]))
    pre = jnp.einsum('std,dce->stce', normed, w_qkv, precision=HIGHEST_PREC) + b_qkv
    pre = low_back(pre).reshape(slots, SLOT, 3, HEADS, HD)
    mixed = lax.map(jax.checkpoint(attend), (pre, lengths))
    mixed = low_back(low(mixed.reshape(slots, SLOT, D)))
    attn_part = jnp.einsum('ste,ed->std', mixed, w_attn_out, precision=HIGHEST_PREC)
    normed_two = low(layer_norm(acts, gains[1], shifts[1]))
    hidden = low_back(jnp.einsum('std,df->stf', normed_two, w_in, precision=HIGHEST_PREC) + b_in)
    activated = low(jax.nn.gelu(hidden, approximate=False))
    mlp_part = jnp.einsum('stf,fd->std', activated, w_out, precision=HIGHEST_PREC)
    return acts + attn_part + mlp_part + b_out

def reference(inputs, cotangent, seq_lengths, w_qkv, b_qkv, w_attn_out, w_in, b_in, w_out, b_out, norm_gains, norm_biases):
    slots = MB * N_DP
    start_acts = inputs.astype(jnp.float32).reshape(slots, SLOT, D)
    lengths = seq_lengths.reshape(slots, SEQS).astype(jnp.int32)
    params = (w_qkv.astype(jnp.float32), b_qkv.astype(jnp.float32), w_attn_out.astype(jnp.float32), w_in.astype(jnp.float32), b_in.astype(jnp.float32), w_out.astype(jnp.float32), b_out.astype(jnp.float32), norm_gains.astype(jnp.float32), norm_biases.astype(jnp.float32))

    def forward(acts, probe, weights):
        first = layer(acts, lengths, *[entry[0] for entry in weights])
        passed = low_back(low(first)) + probe
        last = layer(passed, lengths, *[entry[1] for entry in weights])
        return (last, first)
    last, pullback, first = jax.vjp(forward, start_acts, jnp.zeros_like(start_acts), params, has_aux=True)
    grad_acts, grad_probe, grads = pullback(cotangent.astype(jnp.float32).reshape(slots, SLOT, D))
    section_out = jnp.stack([first, last]).reshape(2, MB, TOKENS, D).astype(jnp.bfloat16)
    input_grads = jnp.stack([grad_acts, grad_probe]).reshape(2, MB, TOKENS, D).astype(jnp.bfloat16)
    return (section_out, input_grads, grads[0], grads[1], grads[2], grads[3], grads[4], grads[5], grads[6], grads[7], grads[8])
```

```python
import functools
import math

import jax
import jax.numpy as jnp
from jax import lax
from jax.experimental import pallas as pl
from jax.experimental.pallas import tpu as pltpu
from jax.sharding import PartitionSpec as P

HD = 64
ROT = 16
BLOCK = 128
SEQS = 4
SLOT = 512
D = 768
LOCAL = 192
EPSILON = 1e-05
MASKED = -1e30
MESH = pl.DeviceIdType.MESH
BF = jnp.bfloat16
F32 = jnp.float32
VMEM_LIMIT = 56 * 2**20


def coords():
    dp = lax.axis_index("dp")
    return (
        lax.axis_index("section"),
        dp // 4,
        (dp // 2) % 2,
        dp % 2,
        lax.axis_index("tensor"),
    )


def dp_of(y, x, c):
    return y * 4 + x * 2 + c


def signal_all(targets):
    barrier = pltpu.get_barrier_semaphore()
    for target in targets:
        pl.semaphore_signal(barrier, inc=1, device_id=target, device_id_type=MESH)
    pl.semaphore_wait(barrier, len(targets))


def remote(src, dst, send, recv, target):
    return pltpu.make_async_remote_copy(
        src_ref=src,
        dst_ref=dst,
        send_sem=send,
        recv_sem=recv,
        device_id=target,
        device_id_type=MESH,
    )


def gather_kernel(shard_ref, vec_ref, w_ref, vecs_ref, send, recv, xsend, xrecv):
    s, y, x, c, _ = coords()
    me = dp_of(y, x, c)
    to_y = [{"dp": dp_of((y + k) % 4, x, c)} for k in (1, 2, 3)]
    to_x = {"dp": dp_of(y, 1 - x, c)}
    to_c = {"dp": dp_of(y, x, 1 - c)}
    to_s = {"section": 1 - s}
    signal_all(to_y + [to_x, to_c, to_s])
    w_ref[s, :, me] = shard_ref[...]
    vecs_ref[s] = vec_ref[...]

    def swap(layer, to):
        return [
            remote(w_ref.at[layer, :, me], w_ref.at[layer, :, me], xsend.at[0], xrecv.at[0], to),
            remote(vecs_ref.at[layer], vecs_ref.at[layer], xsend.at[1], xrecv.at[1], to),
        ]

    sent = []

    def push(order, layer, chunk, slot, block, to):
        number = (order * 3 + chunk) * 15 + slot
        copy = remote(
            w_ref.at[layer, chunk, block],
            w_ref.at[layer, chunk, block],
            send.at[number],
            recv.at[number],
            to,
        )
        copy.start()
        sent.append(copy)

    def arrived(order, layer, chunk, slot, block):
        number = (order * 3 + chunk) * 15 + slot
        remote(
            w_ref.at[layer, chunk, block],
            w_ref.at[layer, chunk, block],
            send.at[number],
            recv.at[number],
            to_c,
        ).wait_recv()

    def block_of(j, other):
        return dp_of((y + 4 - j) % 4, (1 - x) if other else x, c)

    def sib_block(j, other):
        return dp_of((y + 4 - j) % 4, (1 - x) if other else x, 1 - c)

    def first(order, layer):
        for chunk in range(3):
            if chunk < 2:
                for k in (1, 2, 3):
                    push(order, layer, chunk, k - 1, me, to_y[k - 1])
                push(order, layer, chunk, 3, me, to_x)
            else:
                push(order, layer, chunk, 0, me, to_x)
                for k in (1, 2, 3):
                    push(order, layer, chunk, k, me, to_y[k - 1])
            push(order, layer, chunk, 7, me, to_c)

    def second(order, layer):
        for chunk in (2, 0, 1):
            if chunk == 2:
                arrived(order, layer, chunk, 0, block_of(0, True))
                for k in (1, 2, 3):
                    push(order, layer, chunk, 3 + k, block_of(0, True), to_y[k - 1])
                push(order, layer, chunk, 8, block_of(0, True), to_c)
            else:
                for j in (1, 3, 2):
                    arrived(order, layer, chunk, j - 1, block_of(j, False))
                    push(order, layer, chunk, 3 + j, block_of(j, False), to_x)
                    push(order, layer, chunk, 7 + 2 * j, block_of(j, False), to_c)

    def third(order, layer):
        for chunk in (0, 1, 2):
            if chunk < 2:
                for j in (0, 1, 3, 2):
                    arrived(order, layer, chunk, 3 + j, block_of(j, True))
                    push(order, layer, chunk, 8 + 2 * j, block_of(j, True), to_c)
            else:
                for j in (1, 3, 2):
                    arrived(order, layer, chunk, j, block_of(j, False))
                    push(order, layer, chunk, 7 + 2 * j, block_of(j, False), to_c)
                for j in (1, 3, 2):
                    arrived(order, layer, chunk, 3 + j, block_of(j, True))
                    push(order, layer, chunk, 8 + 2 * j, block_of(j, True), to_c)

    def fourth(order, layer):
        for chunk in range(3):
            for j in range(4):
                arrived(order, layer, chunk, 7 + 2 * j, sib_block(j, False))
                arrived(order, layer, chunk, 8 + 2 * j, sib_block(j, True))

    outgoing = swap(s, to_s)
    for copy in outgoing:
        copy.start()
    first(0, s)
    second(0, s)
    for copy in swap(1 - s, to_s):
        copy.wait_recv()
    first(1, 1 - s)
    third(0, s)
    second(1, 1 - s)
    third(1, 1 - s)
    fourth(0, s)
    fourth(1, 1 - s)
    for copy in outgoing + sent:
        copy.wait_send()


def gather(shard, vec):
    dma = pltpu.SemaphoreType.DMA
    vmem = pl.BlockSpec(memory_space=pltpu.VMEM)
    return pl.pallas_call(
        gather_kernel,
        out_shape=[
            jax.ShapeDtypeStruct((2, 3, 16, 48, D), BF),
            jax.ShapeDtypeStruct((2, 8, D), F32),
        ],
        in_specs=[vmem, vmem],
        out_specs=[vmem, vmem],
        scratch_shapes=[dma((90,)), dma((90,)), dma((2,)), dma((2,))],
        compiler_params=pltpu.CompilerParams(
            collective_id=0, has_side_effects=True, vmem_limit_bytes=VMEM_LIMIT
        ),
        name="weights_gather",
    )(shard, vec)


def tensor_kernel(whole, part_ref, extra_ref, out_ref, landed, send, recv):
    t = lax.axis_index("tensor")
    to = [{"tensor": (t + k) % 4} for k in (1, 2, 3)]
    signal_all(to)
    copies = []
    for k in (1, 3, 2):
        copy = remote(
            part_ref.at[(t + k) % 4], landed.at[k - 1], send.at[k - 1], recv.at[k - 1], to[k - 1]
        )
        copy.start()
        copies.append(copy)
    for copy in copies:
        copy.wait_recv()
    rows = part_ref.shape[1]

    def add(i, _):
        at = pl.ds(pl.multiple_of(i * 32, 32), 32)
        total = extra_ref[at, :] + part_ref[t, at, :].astype(F32)
        for k in range(3):
            total = total + landed[k, at, :].astype(F32)
        if whole:
            out_ref[t, at, :] = total.astype(BF)
        else:
            out_ref[at, :] = total.astype(BF)
        return 0

    lax.fori_loop(0, rows // 32, add, 0)
    if whole:
        spread = []
        for k in (1, 3, 2):
            copy = remote(
                out_ref.at[t], out_ref.at[t], send.at[2 + k], recv.at[2 + k], to[k - 1]
            )
            copy.start()
            spread.append(copy)
        for k in (1, 3, 2):
            source = (t + 4 - k) % 4
            remote(
                out_ref.at[source], out_ref.at[source], send.at[2 + k], recv.at[2 + k], to[0]
            ).wait_recv()
        copies += spread
    for copy in copies:
        copy.wait_send()


def tensor_sum(number, whole, parts, extra):
    dma = pltpu.SemaphoreType.DMA
    vmem = pl.BlockSpec(memory_space=pltpu.VMEM)
    _, rows, cols = parts.shape
    return pl.pallas_call(
        functools.partial(tensor_kernel, whole),
        out_shape=jax.ShapeDtypeStruct((4, rows, cols) if whole else (rows, cols), BF),
        in_specs=[vmem, vmem],
        out_specs=vmem,
        scratch_shapes=[pltpu.VMEM((3, rows, cols), BF), dma((6,)), dma((6,))],
        compiler_params=pltpu.CompilerParams(
            collective_id=number, has_side_effects=True, vmem_limit_bytes=VMEM_LIMIT
        ),
        name="tensor_sum",
    )(parts, extra)


def reduce_kernel(
    g_ref,
    va_ref,
    vb_ref,
    acts_ref,
    w_out,
    va_out,
    vb_out,
    acts_out,
    sib,
    xbuf,
    ybuf,
    sbuf,
    stage,
    keep,
    vland,
    vsum,
    send,
    recv,
    vsend,
    vrecv,
    asend,
    arecv,
):
    s, y, x, c, t = coords()
    to_y = [{"dp": dp_of((y + k) % 4, x, c)} for k in (1, 2, 3)]
    to_z = [{"tensor": (t + k) % 4} for k in (1, 2, 3)]
    to_x = {"dp": dp_of(y, 1 - x, c)}
    to_c = {"dp": dp_of(y, x, 1 - c)}
    to_s = {"section": 1 - s}
    signal_all(to_y + to_z + [to_x, to_c, to_s])
    sent = []

    def start(src, dst, number, to, sems=(send, recv)):
        copy = remote(src, dst, sems[0].at[number], sems[1].at[number], to)
        copy.start()
        sent.append(copy)

    def landed(ref, number, sems=(send, recv)):
        remote(ref, ref, sems[0].at[number], sems[1].at[number], to_c).wait_recv()

    start(acts_ref.at[1 - s], acts_out.at[s], 0, to_s, (asend, arecv))
    acts_out[s] = acts_ref[s]

    for layer in (1, 0):
        for chunk in range(3):
            start(g_ref.at[layer, chunk, :, 1 - c], sib.at[layer, chunk], layer * 3 + chunk, to_c)

    def base(layer, chunk):
        return 6 + (layer * 3 + chunk) * 5

    vs = (vsend, vrecv)
    vsum[0:8] = va_ref[...]
    vland[t, 0:8] = vb_ref[...]
    for k in (1, 2, 3):
        start(vb_ref, vland.at[t, pl.ds(0, 8)], k - 1, to_z[k - 1], vs)

    for layer in (1, 0):
        for chunk in range(3):
            landed(sib.at[layer, chunk], layer * 3 + chunk)

            def add(i, _):
                sib[layer, chunk, i] = (
                    sib[layer, chunk, i].astype(F32) + g_ref[layer, chunk, i, c].astype(F32)
                ).astype(BF)
                return 0

            lax.fori_loop(0, 8, add, 0)
            if chunk < 2:
                for j in range(4):
                    yy = (y + j) % 4
                    start(
                        sib.at[layer, chunk, yy * 2 + 1 - x],
                        xbuf.at[layer, chunk, yy],
                        base(layer, chunk) + j,
                        to_x,
                    )
            else:
                for k in (1, 3, 2):
                    yy = (y + k) % 4
                    start(
                        sib.at[layer, chunk, pl.ds(yy * 2, 2)],
                        ybuf.at[layer, pl.ds(2 * (k - 1), 2)],
                        base(layer, chunk) + k - 1,
                        to_y[k - 1],
                    )

    for k in (1, 2, 3):
        landed(vland.at[(t + 4 - k) % 4, pl.ds(0, 8)], k - 1, vs)
    vsum[8:16] = vland[0, 0:8] + vland[1, 0:8] + vland[2, 0:8] + vland[3, 0:8]
    stage[0] = vsum[...]
    start(stage.at[0], vland.at[4], 3, to_c, vs)

    for layer in (1, 0):
        for chunk in range(2):
            for j in range(4):
                yy = (y + j) % 4
                landed(xbuf.at[layer, chunk, yy], base(layer, chunk) + j)
                mine = yy * 2 + x
                xbuf[layer, chunk, yy] = (
                    sib[layer, chunk, mine].astype(F32) + xbuf[layer, chunk, yy].astype(F32)
                ).astype(BF)
            for k in (1, 3, 2):
                yy = (y + k) % 4
                start(
                    xbuf.at[layer, chunk, yy],
                    ybuf.at[layer, 6 + chunk * 3 + k - 1],
                    36 + (layer * 2 + chunk) * 3 + k - 1,
                    to_y[k - 1],
                )
        for k in (1, 3, 2):
            landed(ybuf.at[layer, pl.ds(2 * (k - 1), 2)], base(layer, 2) + k - 1)
        for i in range(2):
            total = sib[layer, 2, y * 2 + i].astype(F32)
            for k in range(3):
                total = total + ybuf[layer, 2 * k + i].astype(F32)
            keep[layer, i] = total.astype(BF)
        start(keep.at[layer, 1 - x], keep.at[layer, 2], 48 + layer, to_x)

    landed(vland.at[4], 3, vs)
    vsum[...] = stage[0] + vland[4]
    stage[1] = vsum[...]
    start(stage.at[1], vland.at[5], 4, to_x, vs)

    def finish(layer):
        for chunk in range(2):
            total = xbuf[layer, chunk, y].astype(F32)
            for k in (1, 3, 2):
                landed(
                    ybuf.at[layer, 6 + chunk * 3 + k - 1], 36 + (layer * 2 + chunk) * 3 + k - 1
                )
            for k in range(3):
                total = total + ybuf[layer, 6 + chunk * 3 + k].astype(F32)
            sbuf[layer, chunk] = total.astype(BF)
        landed(keep.at[layer, 2], 48 + layer)
        sbuf[layer, 2] = (keep[layer, x].astype(F32) + keep[layer, 2].astype(F32)).astype(BF)

    finish(1 - s)
    start(sbuf.at[1 - s], sbuf.at[2], 50, to_s)

    landed(vland.at[5], 4, vs)
    vsum[...] = stage[1] + vland[5]
    stage[2] = vsum[...]
    start(stage.at[2], vland.at[6], 5, to_s, vs)

    finish(s)

    landed(vland.at[6], 5, vs)
    vsum[...] = stage[2] + vland[6]
    stage[3] = vsum[...]
    vland[7 + y] = vsum[...]
    for k in (1, 2, 3):
        start(stage.at[3], vland.at[7 + y], 5 + k, to_y[k - 1], vs)

    landed(sbuf.at[2], 50)
    for chunk in range(3):
        w_out[chunk] = sbuf[s, chunk].astype(F32) + sbuf[2, chunk].astype(F32)

    for k in (1, 2, 3):
        landed(vland.at[7 + (y + 4 - k) % 4], 5 + k, vs)
    vsum[...] = vland[7] + vland[8] + vland[9] + vland[10]
    va_out[...] = vsum[0:8]
    vb_out[...] = vsum[8:16]
    landed(acts_out.at[1 - s], 0, (asend, arecv))
    for copy in sent:
        copy.wait_send()


def reduce_all(grads, va, vb, acts):
    dma = pltpu.SemaphoreType.DMA
    vmem = pl.BlockSpec(memory_space=pltpu.VMEM)
    return pl.pallas_call(
        reduce_kernel,
        out_shape=[
            jax.ShapeDtypeStruct((3, 48, D), F32),
            jax.ShapeDtypeStruct((8, D), F32),
            jax.ShapeDtypeStruct((8, D), F32),
            jax.ShapeDtypeStruct(acts.shape, BF),
        ],
        in_specs=[vmem] * 4,
        out_specs=[vmem] * 4,
        scratch_shapes=[
            pltpu.VMEM((2, 3, 8, 48, D), BF),
            pltpu.VMEM((2, 2, 4, 48, D), BF),
            pltpu.VMEM((2, 12, 48, D), BF),
            pltpu.VMEM((3, 3, 48, D), BF),
            pltpu.VMEM((4, 16, D), F32),
            pltpu.VMEM((2, 3, 48, D), BF),
            pltpu.VMEM((11, 16, D), F32),
            pltpu.VMEM((16, D), F32),
            dma((51,)),
            dma((51,)),
            dma((9,)),
            dma((9,)),
            dma((1,)),
            dma((1,)),
        ],
        compiler_params=pltpu.CompilerParams(
            collective_id=3, has_side_effects=True, vmem_limit_bytes=VMEM_LIMIT
        ),
        name="grads_reduce",
    )(grads, va, vb, acts)


def arrange(lengths):
    blocks = (lengths + BLOCK - 1) // BLOCK
    block_ends = jnp.cumsum(blocks)
    places = jnp.arange(SLOT, dtype=jnp.int32)
    owners = jnp.sum((block_ends[None, :] <= (places // BLOCK)[:, None]).astype(jnp.int32), axis=1)
    starts = jnp.concatenate([jnp.zeros((1,), jnp.int32), block_ends]) * BLOCK
    limits = jnp.concatenate([lengths, jnp.zeros((1,), jnp.int32)])
    chosen = (owners[:, None] == jnp.arange(SEQS + 1, dtype=jnp.int32)[None, :]).astype(jnp.int32)
    offset = places - jnp.sum(chosen * starts[None, :], axis=1)
    seq_len = jnp.sum(chosen * limits[None, :], axis=1)
    allowed = (
        (owners[:, None] == owners[None, :])
        & (offset[None, :] <= offset[:, None])
        & ((offset[None, :] < seq_len[None, :]) | (places[:, None] == places[None, :]))
    )
    half_rot = ROT // 2
    inv_freq = 1.0 / 10000.0 ** (jnp.arange(half_rot, dtype=jnp.float32) * 2.0 / ROT)
    angles = offset.astype(jnp.float32)[:, None] * inv_freq[None, :]
    return (jnp.cos(angles), jnp.sin(angles), allowed)


def rotate(values, cosines, sines):
    half_rot = ROT // 2
    cos_rows = cosines[:, None, :]
    sin_rows = sines[:, None, :]
    first = values[..., :half_rot]
    second = values[..., half_rot:ROT]
    return jnp.concatenate(
        [
            first * cos_rows - second * sin_rows,
            second * cos_rows + first * sin_rows,
            values[..., ROT:],
        ],
        axis=-1,
    )


def dot(a, b):
    return jnp.dot(a, b, preferred_element_type=F32)


def dot_nt(a, b):
    return lax.dot_general(a, b, (((1,), (1,)), ((), ())), preferred_element_type=F32)


def dot_tn(a, b):
    return lax.dot_general(a, b, (((0,), (0,)), ((), ())), preferred_element_type=F32)


def gelu_exact(values):
    return jax.nn.gelu(values, approximate=False)


def normalize(acts):
    average = jnp.mean(acts, axis=-1, keepdims=True)
    centred = acts - average
    spread = jnp.mean(centred * centred, axis=-1, keepdims=True)
    rstd = lax.rsqrt(spread + EPSILON)
    return centred * rstd, rstd


def forward(acts_bf, w, vec, seq):
    cosines, sines, allowed = seq
    w_in, w_out_t, w_c = w[0], w[1], w[2]
    normal, rstd = normalize(acts_bf.astype(F32))
    normed = (normal * vec[3] + vec[5]).astype(BF)
    pre = (dot(normed, w_c[:, : 3 * LOCAL]) + vec[0, : 3 * LOCAL]).reshape(SLOT, 3, 3, HD)
    query = rotate(pre[:, 0], cosines, sines).astype(BF)
    key = rotate(pre[:, 1], cosines, sines).astype(BF)
    value = pre[:, 2].astype(BF)
    scores = jnp.einsum("qhd,khd->hqk", query, key, preferred_element_type=F32) / math.sqrt(HD)
    masked = jnp.where(allowed[None], scores, MASKED)
    top = jnp.max(masked, axis=-1, keepdims=True)
    weights = jnp.where(allowed[None], jnp.exp(masked - top), 0.0)
    probs_f = weights / jnp.sum(weights, axis=-1, keepdims=True)
    probs = probs_f.astype(BF)
    mixed = (
        jnp.einsum("hqk,khd->qhd", probs, value, preferred_element_type=F32)
        .reshape(SLOT, LOCAL)
        .astype(BF)
    )
    normed_two = (normal * vec[4] + vec[6]).astype(BF)
    hidden = dot(normed_two, w_in) + vec[1]
    activated = gelu_exact(hidden).astype(BF)
    part = dot_nt(mixed, w_c[:, 3 * LOCAL :]) + dot_nt(activated, w_out_t)
    kept = (normal, rstd, normed, query, key, value, probs_f, mixed, normed_two, hidden, activated)
    return part.astype(BF), kept


def backward(grad, kept, w, vec, seq):
    normal, rstd, normed, query, key, value, probs_f, mixed, normed_two, hidden, activated = kept
    cosines, sines, _ = seq
    w_in, w_out_t, w_c = w[0], w[1], w[2]
    g_out_bias = jnp.sum(grad.astype(F32), axis=0)
    grad_mixed = dot(grad, w_c[:, 3 * LOCAL :]).astype(BF).reshape(SLOT, 3, HD)
    g_attn = dot_tn(grad, mixed)
    g_out = dot_tn(grad, activated)
    grad_act = dot(grad, w_out_t)
    grad_hidden = jax.vjp(gelu_exact, hidden)[1](grad_act)[0].astype(BF)
    g_in_bias = jnp.sum(grad_hidden.astype(F32), axis=0)
    g_in = dot_tn(normed_two, grad_hidden)
    grad_norm_two = dot_nt(grad_hidden, w_in)
    grad_probs = jnp.einsum("qhd,khd->hqk", grad_mixed, value, preferred_element_type=F32)
    row_dot = jnp.sum(probs_f * grad_probs, axis=-1, keepdims=True)
    grad_scores = (probs_f * (grad_probs - row_dot)).astype(BF)
    scale = 1.0 / math.sqrt(HD)
    grad_query = jnp.einsum("hqk,khd->qhd", grad_scores, key, preferred_element_type=F32) * scale
    grad_key = jnp.einsum("hqk,qhd->khd", grad_scores, query, preferred_element_type=F32) * scale
    grad_value = jnp.einsum(
        "hqk,qhd->khd", probs_f.astype(BF), grad_mixed, preferred_element_type=F32
    )
    grad_pre = jnp.stack(
        [rotate(grad_query, cosines, -sines), rotate(grad_key, cosines, -sines), grad_value],
        axis=1,
    )
    grad_pre = grad_pre.reshape(SLOT, 3 * LOCAL).astype(BF)
    g_qkv_bias = jnp.sum(grad_pre.astype(F32), axis=0)
    g_qkv = dot_tn(normed, grad_pre)
    grad_normed = dot_nt(grad_pre, w_c[:, : 3 * LOCAL])
    mixture = grad_normed * vec[3] + grad_norm_two * vec[4]
    part = rstd * (
        mixture
        - jnp.mean(mixture, axis=-1, keepdims=True)
        - normal * jnp.mean(mixture * normal, axis=-1, keepdims=True)
    )
    weights = jnp.stack([g_in, g_out, jnp.concatenate([g_qkv, g_attn], axis=1)]).astype(BF)
    zero = jnp.zeros((D,), F32)
    va = jnp.stack(
        [jnp.concatenate([g_qkv_bias, jnp.zeros((LOCAL,), F32)]), g_in_bias, g_out_bias, zero]
    )
    vb = jnp.stack(
        [
            jnp.sum(grad_normed * normal, axis=0),
            jnp.sum(grad_norm_two * normal, axis=0),
            jnp.sum(grad_normed, axis=0),
            jnp.sum(grad_norm_two, axis=0),
        ]
    )
    return part.astype(BF), weights.reshape(3, 8, 2, 48, D), va, vb


def columns(values, t):
    mine = lax.dynamic_slice_in_dim(values, t * LOCAL, LOCAL, 1)
    return mine.reshape(2, 256, LOCAL).transpose(1, 0, 2).reshape(256, 2 * LOCAL)


def column_blocks(part):
    return part.reshape(2, 256, 4, LOCAL).transpose(2, 1, 0, 3).reshape(4, 256, 2 * LOCAL)


def body(
    inputs,
    cotangent,
    seq_lengths,
    w_qkv,
    b_qkv,
    w_attn_out,
    w_in,
    b_in,
    w_out,
    b_out,
    norm_gains,
    norm_biases,
):
    s = lax.axis_index("section")
    t = lax.axis_index("tensor")
    shard = jnp.stack(
        [
            w_in[0],
            w_out[0].T,
            jnp.concatenate([w_qkv[0].reshape(48, 3 * LOCAL), w_attn_out[0].T], axis=1),
        ]
    )
    vec = jnp.concatenate(
        [
            jnp.pad(b_qkv[0].reshape(1, -1), ((0, 0), (0, LOCAL))),
            b_in,
            b_out,
            norm_gains[0],
            norm_biases[0],
            jnp.zeros((1, D), F32),
        ]
    )
    weights, vecs = gather(shard, vec)
    weights = weights.reshape(2, 3, D, D)

    acts = lax.dynamic_index_in_dim(inputs, s, 0, keepdims=False)
    grad = lax.dynamic_index_in_dim(cotangent, s, 0, keepdims=False)
    lengths = lax.dynamic_index_in_dim(seq_lengths[:, 0], s, 0, keepdims=False)
    seq = arrange(lengths)

    zero_vec, one_vec = vecs[0], vecs[1]
    part, kept_zero = forward(acts, weights[0], zero_vec, seq)
    own = lax.dynamic_slice_in_dim(acts, t * 128, 128, 0).astype(F32) + zero_vec[2]
    acts_one = tensor_sum(1, True, part.reshape(4, 128, D), own).reshape(SLOT, D)
    part, kept_one = forward(acts_one, weights[1], one_vec, seq)
    bias_cols = lax.dynamic_slice_in_dim(one_vec[2], t * LOCAL, LOCAL, 0)
    extra = columns(acts_one, t).astype(F32) + jnp.tile(bias_cols, 2)
    acts_two = tensor_sum(2, False, column_blocks(part), extra)

    part, w_grads_one, va_one, vb_one = backward(grad, kept_one, weights[1], one_vec, seq)
    own = lax.dynamic_slice_in_dim(grad, t * 128, 128, 0).astype(F32)
    grad_one = tensor_sum(4, True, part.reshape(4, 128, D), own).reshape(SLOT, D)
    part, w_grads_zero, va_zero, vb_zero = backward(grad_one, kept_zero, weights[0], zero_vec, seq)
    grad_zero = tensor_sum(
        5, False, column_blocks(part), columns(grad_one, t).astype(F32)
    )
    outs = jnp.stack(
        [
            jnp.stack([columns(acts_one, t), grad_zero]),
            jnp.stack([acts_two, columns(grad_one, t)]),
        ]
    )
    w_sums, va, vb, acts_all = reduce_all(
        jnp.stack([w_grads_zero, w_grads_one]),
        jnp.concatenate([va_zero, va_one]),
        jnp.concatenate([vb_zero, vb_one]),
        outs,
    )
    acts_all = acts_all.reshape(2, 2, 256, 2, LOCAL).transpose(0, 1, 3, 2, 4)
    acts_all = acts_all.reshape(2, 2, SLOT, LOCAL)
    va = lax.dynamic_slice_in_dim(va, s * 4, 4, 0)
    vb = lax.dynamic_slice_in_dim(vb, s * 4, 4, 0)
    return (
        acts_all[:, 0][None],
        acts_all[:, 1][None],
        w_sums[2, :, : 3 * LOCAL].reshape(1, 48, 3, LOCAL),
        va[0, : 3 * LOCAL].reshape(1, 3, LOCAL),
        w_sums[2, :, 3 * LOCAL :].T[None],
        w_sums[0][None],
        va[1][None],
        w_sums[1].T[None],
        va[2][None],
        vb[0:2][None],
        vb[2:4][None],
    )


def solution(mesh):
    return jax.shard_map(
        body,
        mesh=mesh,
        in_specs=(
            P(None, "dp", None),
            P(None, "dp", None),
            P(None, "dp", None),
            P("section", "dp", None, "tensor"),
            P("section", None, "tensor"),
            P("section", "tensor", "dp"),
            P("section", "dp", "tensor"),
            P("section", "tensor"),
            P("section", "tensor", "dp"),
            P("section", None),
            P("section", None, None),
            P("section", None, None),
        ),
        out_specs=(
            P("section", None, "dp", "tensor"),
            P("section", None, "dp", "tensor"),
            P("section", "dp", None, "tensor"),
            P("section", None, "tensor"),
            P("section", "tensor", "dp"),
            P("section", "dp", "tensor"),
            P("section", "tensor"),
            P("section", "tensor", "dp"),
            P("section", None),
            P("section", None, None),
            P("section", None, None),
        ),
        check_vma=False,
    )
```

```python
import math

import jax
import jax.numpy as jnp
import numpy as np
from jax import lax
from jax.experimental import pallas as pl
from jax.experimental.pallas import tpu as pltpu
from jax.sharding import PartitionSpec as P

HD = 64
ROT = 16
BLOCK = 128
SEQS = 4
SLOT = 512
D = 768
LOCAL = 192
EPSILON = 1e-05
MASKED = -1e30
MESH = pl.DeviceIdType.MESH
BF = jnp.bfloat16
F32 = jnp.float32
VMEM_LIMIT = 58 * 2**20


def coords():
    dp = lax.axis_index("dp")
    return (
        lax.axis_index("section"),
        dp // 4,
        (dp // 2) % 2,
        dp % 2,
        lax.axis_index("tensor"),
    )


def dp_of(y, x, c):
    return y * 4 + x * 2 + c


def signal_all(targets):
    barrier = pltpu.get_barrier_semaphore()
    for target in targets:
        pl.semaphore_signal(barrier, inc=1, device_id=target, device_id_type=MESH)
    pl.semaphore_wait(barrier, len(targets))


def remote(src, dst, send, recv, target):
    return pltpu.make_async_remote_copy(
        src_ref=src,
        dst_ref=dst,
        send_sem=send,
        recv_sem=recv,
        device_id=target,
        device_id_type=MESH,
    )


def dot(a, b):
    return lax.dot_general(a, b, (((1,), (0,)), ((), ())), preferred_element_type=F32)


def dot_nt(a, b):
    return lax.dot_general(a, b, (((1,), (1,)), ((), ())), preferred_element_type=F32)


def dot_tn(a, b):
    return lax.dot_general(a, b, (((0,), (0,)), ((), ())), preferred_element_type=F32)


def gelu_parts(h):
    tail = 1.0 / (1.0 + (0.3275911 / math.sqrt(2.0)) * jnp.abs(h))
    bell = jnp.exp(h * h * -0.5)
    series = 0.5 * 1.061405429
    for term in (-1.453152027, 1.421413741, -0.284496736, 0.254829592):
        series = series * tail + 0.5 * term
    below = series * tail * bell
    phi = jnp.where(h >= 0.0, 1.0 - below, below)
    return h * phi, phi + h * bell * (1.0 / math.sqrt(2.0 * math.pi))


def col_sum(values):
    return jnp.sum(values, axis=0, keepdims=True)


class Copies:
    def __init__(self, send, recv, to_any):
        self.send, self.recv, self.to_any = send, recv, to_any
        self.numbers = {}
        self.sent = []
        self.done = set()

    def make(self, name, src, dst, to):
        number = self.numbers.setdefault(name, len(self.numbers))
        assert number < SEMS
        return remote(src, dst, self.send.at[number], self.recv.at[number], to)

    def start(self, name, src, dst, to):
        copy = self.make(name, src, dst, to)
        copy.start()
        self.late(name, copy)

    def late(self, name, copy):
        self.sent.append((self.numbers[name], copy))

    def landed(self, name, ref):
        self.make(name, ref, ref, self.to_any).wait_recv()

    def sent_off(self, name, src, dst, to):
        copy = self.make(name, src, dst, to)
        copy.wait_send()
        self.done.add(self.numbers[name])

    def finish(self):
        for number, copy in self.sent:
            if number not in self.done:
                copy.wait_send()


SEMS = 240


def mega_kernel(
    len_ref,
    freq_ref,
    inputs_ref,
    cot_ref,
    wqkv_ref,
    wattn_ref,
    win_ref,
    wout_ref,
    bqkv_ref,
    bin_ref,
    bout_ref,
    gains_ref,
    shifts_ref,
    sec_out,
    grad_out,
    w_out,
    va_out,
    vb_out,
    w,
    vecs,
    x0,
    x1,
    g1,
    g0,
    tables,
    bias,
    normal,
    rstd,
    na,
    nb,
    q,
    k,
    v,
    probs,
    mixp,
    act,
    slope,
    gm,
    gh,
    dqk,
    dv,
    gpre,
    full,
    zrow,
    zcol,
    zland,
    zland_c,
    acts,
    acts_in,
    grads,
    sib,
    xbuf,
    ybuf,
    keep,
    sbuf,
    sbuf_in,
    vec,
    vland,
    stage,
    send,
    recv,
    local,
):
    s, y, x, c, t = coords()
    me = dp_of(y, x, c)
    to_y = {j: {"dp": dp_of((y + j) % 4, x, c)} for j in (1, 2, 3)}
    to_z = {j: {"tensor": (t + j) % 4} for j in (1, 2, 3)}
    to_x = {"dp": dp_of(y, 1 - x, c)}
    to_c = {"dp": dp_of(y, x, 1 - c)}
    to_s = {"section": 1 - s}
    cp = Copies(send, recv, to_c)

    fetch_x = pltpu.make_async_copy(inputs_ref.at[s], x0, local.at[0])
    fetch_g = pltpu.make_async_copy(cot_ref.at[s], g1, local.at[1])
    fetch_x.start()
    fetch_g.start()

    def rows48(block):
        return pl.ds(pl.multiple_of(block * 48, 16), 48)

    eye = (
        lax.broadcasted_iota(jnp.int32, (48, 48), 0) == lax.broadcasted_iota(jnp.int32, (48, 48), 1)
    ).astype(BF)
    w[s, 0, rows48(me), :] = win_ref[...]
    w[s, 1, rows48(me), :] = dot_nt(eye, wout_ref[...]).astype(BF)
    w[s, 2, rows48(me), :] = jnp.concatenate(
        [wqkv_ref[...], dot_nt(eye, wattn_ref[...]).astype(BF)], axis=1
    )
    vecs[s, 0:1, :] = bqkv_ref[...]
    vecs[s, 1:2, :] = bin_ref[...]
    vecs[s, 2:3, :] = bout_ref[...]
    vecs[s, 3:5, :] = gains_ref[...]
    vecs[s, 5:7, :] = shifts_ref[...]
    vecs[s, 7:8, :] = jnp.zeros((1, D), F32)

    signal_all(list(to_y.values()) + list(to_z.values()) + [to_x, to_c, to_s])

    cp.start("swap_w", w.at[s, :, rows48(me)], w.at[s, :, rows48(me)], to_s)
    cp.start("swap_v", vecs.at[s], vecs.at[s], to_s)

    def swapped():
        cp.landed("swap_w", w.at[1 - s, :, rows48(me)])
        cp.landed("swap_v", vecs.at[1 - s])

    def block_of(j, other, core=c):
        return dp_of((y + 4 - j) % 4, (1 - x) if other else x, core)

    def push(l, ch, slot, block, to):
        ref = w.at[l, ch, rows48(block)]
        cp.start(("w", l, ch, slot), ref, ref, to)

    def arrived(l, ch, slot, block):
        cp.landed(("w", l, ch, slot), w.at[l, ch, rows48(block)])

    def gather_first(l):
        for ch in (2, 0, 1):
            if ch < 2:
                for j in (1, 3, 2):
                    push(l, ch, j - 1, me, to_y[j])
                push(l, ch, 3, me, to_x)
            else:
                push(l, ch, 0, me, to_x)
                for j in (1, 3, 2):
                    push(l, ch, j, me, to_y[j])
            push(l, ch, 7, me, to_c)

    def gather_second(l):
        for ch in (2, 0, 1):
            if ch == 2:
                arrived(l, ch, 0, block_of(0, True))
                for j in (1, 3, 2):
                    push(l, ch, 3 + j, block_of(0, True), to_y[j])
                push(l, ch, 8, block_of(0, True), to_c)
            else:
                for j in (1, 3, 2):
                    arrived(l, ch, j - 1, block_of(j, False))
                    push(l, ch, 3 + j, block_of(j, False), to_x)
                    push(l, ch, 7 + 2 * j, block_of(j, False), to_c)

    def gather_third(l):
        for ch in (2, 0, 1):
            if ch < 2:
                for j in (0, 1, 3, 2):
                    arrived(l, ch, 3 + j, block_of(j, True))
                    push(l, ch, 8 + 2 * j, block_of(j, True), to_c)
            else:
                for j in (1, 3, 2):
                    arrived(l, ch, j, block_of(j, False))
                    push(l, ch, 7 + 2 * j, block_of(j, False), to_c)
                for j in (1, 3, 2):
                    arrived(l, ch, 3 + j, block_of(j, True))
                    push(l, ch, 8 + 2 * j, block_of(j, True), to_c)

    def gather_fourth(l, chunks=(0, 1, 2)):
        for ch in chunks:
            for j in range(4):
                arrived(l, ch, 7 + 2 * j, block_of(j, False, 1 - c))
                arrived(l, ch, 8 + 2 * j, block_of(j, True, 1 - c))

    def prepare():
        lens = [len_ref[s, j] for j in range(SEQS)]
        ends, total = [], 0
        for j in range(SEQS):
            total = total + ((lens[j] + (BLOCK - 1)) >> 7)
            ends.append(total)

        def rows_of(i, _):
            at = pl.ds(pl.multiple_of(i * 128, 128), 128)
            row = i * 128 + lax.broadcasted_iota(jnp.int32, (128, SLOT), 0)
            col = lax.broadcasted_iota(jnp.int32, (128, SLOT), 1)
            block = i
            begin = jnp.int32(0)
            owner = jnp.int32(0)
            for j in range(SEQS):
                past = (ends[j] <= block).astype(jnp.int32)
                begin = jnp.maximum(begin, past * ends[j])
                owner = owner + past
            begin = begin * BLOCK
            size = jnp.int32(0)
            for j in range(SEQS):
                size = size + (owner == j).astype(jnp.int32) * lens[j]
            fine = (col >= begin) & (col <= row) & (col < begin + size) | (col == row)
            bias[at, :] = jnp.where(fine, 0.0, MASKED)
            offset = (row[:, :128] - begin).astype(F32)
            angles = offset * freq_ref[...]
            lane = lax.broadcasted_iota(jnp.int32, (128, 128), 1) & 63
            cosines, sines = jnp.cos(angles), jnp.sin(angles)
            tables[0, at, :] = jnp.where(lane < ROT, cosines, 1.0)
            tables[1, at, :] = jnp.where(lane < ROT // 2, -sines, 0.0)
            tables[2, at, :] = jnp.where((lane >= ROT // 2) & (lane < ROT), sines, 0.0)
            return 0

        lax.fori_loop(0, 4, rows_of, 0)

    def turn(values, at, sign):
        ahead = pltpu.roll(values, 384 - ROT // 2, 1)
        behind = pltpu.roll(values, ROT // 2, 1)
        parts = []
        for b in range(3):
            lanes = slice(128 * b, 128 * b + 128)
            change = ahead[:, lanes] * tables[1, at, :] + behind[:, lanes] * tables[2, at, :]
            base = values[:, lanes] * tables[0, at, :]
            parts.append(base + change if sign > 0 else base - change)
        return jnp.concatenate(parts, axis=1)

    def norms(l, x_ref):
        def rows_of(i, _):
            at = pl.ds(pl.multiple_of(i * 64, 64), 64)
            values = x_ref[at, :].astype(F32)
            centred = values - jnp.mean(values, axis=-1, keepdims=True)
            scale = lax.rsqrt(jnp.mean(centred * centred, axis=-1, keepdims=True) + EPSILON)
            unit = centred * scale
            normal[l, at, :] = unit
            rstd[l, at, :] = jnp.broadcast_to(scale, (64, 128))
            na[l, at, :] = (unit * vecs[l, 3:4, :] + vecs[l, 5:6, :]).astype(BF)
            nb[l, at, :] = (unit * vecs[l, 4:5, :] + vecs[l, 6:7, :]).astype(BF)
            return 0

        lax.fori_loop(0, SLOT // 64, rows_of, 0)

    stored = [slice(64 * j * (j + 1), 64 * (j + 1) * (j + 2)) for j in range(4)]

    def attend(l):
        def rows_of(i, _):
            at = pl.ds(pl.multiple_of(i * 256, 256), 256)
            pre = dot(na[l, at, :], w[l, 2, :, 0 : 3 * LOCAL]) + vecs[l, 0:1, 0 : 3 * LOCAL]
            turned = turn(pre[:, 0 : 2 * LOCAL], at, 1)
            for h in range(3):
                q[l, h, at, :] = (turned[:, HD * h : HD * h + HD] * (1.0 / 8.0)).astype(BF)
                k[l, h, at, :] = turned[:, LOCAL + HD * h : LOCAL + HD * h + HD].astype(BF)
                v[l, h, at, :] = pre[:, 2 * LOCAL + HD * h : 2 * LOCAL + HD * h + HD].astype(BF)
            return 0

        lax.fori_loop(0, 2, rows_of, 0)
        mixp[l, :, 0:LOCAL] = jnp.zeros((SLOT, LOCAL), BF)
        for j in range(4):
            rows = slice(128 * j, 128 * j + 128)
            seen = slice(0, 128 * j + 128)
            for h in range(3):
                scores = dot_nt(q[l, h, rows, :], k[l, h, seen, :]) + bias[rows, seen]
                weights = jnp.exp(scores - jnp.max(scores, axis=-1, keepdims=True))
                share = weights * (1.0 / jnp.sum(weights, axis=-1, keepdims=True))
                probs[l, h, :, stored[j]] = share
                out = dot(share.astype(BF), v[l, h, seen, :])
                mixp[l, rows, LOCAL + HD * h : LOCAL + HD * h + HD] = out.astype(BF)

    def feed(l):
        def rows_of(i, _):
            at = pl.ds(pl.multiple_of(i * 256, 256), 256)
            for n in range(3):
                lanes = slice(256 * n, 256 * n + 256)
                hidden = dot(nb[l, at, :], w[l, 0, :, lanes]) + vecs[l, 1:2, lanes]
                value, grade = gelu_parts(hidden)
                act[l, at, lanes] = value.astype(BF)
                slope[l, at, lanes] = grade
            return 0

        lax.fori_loop(0, 2, rows_of, 0)

    def result_rows(l, i, emit):
        rows = slice(256 * i, 256 * i + 256)
        for n in range(3):
            lanes = slice(256 * n, 256 * n + 256)
            part = dot_nt(act[l, rows, :], w[l, 1, lanes, :])
            part = part + dot_nt(mixp[l, rows, :], w[l, 2, lanes, 2 * LOCAL :])
            emit(i, lanes, part)

    def emit_row(use):
        def emit(i, lanes, part):
            zrow[use, 2 * i, :, lanes] = part[0:128].astype(BF)
            zrow[use, 2 * i + 1, :, lanes] = part[128:256].astype(BF)

        return emit

    def emit_full(i, lanes, part):
        full[256 * i : 256 * i + 256, lanes] = part.astype(BF)

    def row_push(use, i):
        for j in (1, 3, 2):
            other = (t + j) % 4

            @pl.when(other // 2 == i)
            def _():
                cp.make(
                    ("zr", use, j), zrow.at[use, other], zland.at[use, j - 1], to_z[j]
                ).start()

    def row_finish(use, extra, with_bias, out_ref):
        for j in (1, 3, 2):
            cp.landed(("zr", use, j), zland.at[use, j - 1])
        mine = pl.ds(pl.multiple_of(t * 128, 128), 128)

        def rows_of(i, _):
            at = pl.ds(pl.multiple_of(i * 32, 32), 32)
            here = pl.ds(pl.multiple_of(t * 128 + i * 32, 32), 32)
            total = extra[here, :].astype(F32) + zrow[use, t, at, :].astype(F32)
            if with_bias is not None:
                total = total + vecs[with_bias, 2:3, :]
            for j in range(3):
                total = total + zland[use, j, at, :].astype(F32)
            out_ref[here, :] = total.astype(BF)
            return 0

        lax.fori_loop(0, 4, rows_of, 0)
        for j in (1, 3, 2):
            cp.start(("za", use, j), out_ref.at[mine], out_ref.at[mine], to_z[j])
        for j in (1, 3, 2):
            name = ("zr", use, j)
            cp.late(name, cp.make(name, zrow.at[use, (t + j) % 4], zland.at[use, j - 1], to_z[j]))

    def row_wait(use, out_ref):
        for j in (1, 3, 2):
            theirs = pl.ds(pl.multiple_of(((t + 4 - j) % 4) * 128, 128), 128)
            cp.landed(("za", use, j), out_ref.at[theirs])

    def pack(ref, out):
        for b in range(4):

            @pl.when(t == b)
            def _():
                for i in range(2):
                    out[:, LOCAL * i : LOCAL * i + LOCAL] = ref[
                        256 * i : 256 * i + 256, LOCAL * b : LOCAL * b + LOCAL
                    ]

    def col_push(use):
        for b in range(4):
            for i in range(2):
                zcol[use, b, :, LOCAL * i : LOCAL * i + LOCAL] = full[
                    256 * i : 256 * i + 256, LOCAL * b : LOCAL * b + LOCAL
                ]
        for j in (1, 3, 2):
            cp.start(
                ("zc", use, j), zcol.at[use, (t + j) % 4], zland_c.at[use, j - 1], to_z[j]
            )

    def col_finish(use, extra, bias_cols, out):
        for j in (1, 3, 2):
            cp.landed(("zc", use, j), zland_c.at[use, j - 1])

        def rows_of(i, _):
            at = pl.ds(pl.multiple_of(i * 64, 64), 64)
            total = extra[at, :].astype(F32) + zcol[use, t, at, :].astype(F32)
            if bias_cols:
                total = total + stage[4, 0:1, 0 : 2 * LOCAL]
            for j in range(3):
                total = total + zland_c[use, j, at, :].astype(F32)
            out[at, :] = total.astype(BF)
            return 0

        lax.fori_loop(0, 4, rows_of, 0)

    def act_push(l, kind):
        @pl.when(s == 1 - l)
        def _():
            cp.make(("act", kind), acts.at[l, kind], acts_in.at[kind], to_s).start()

    def back_heads(l, g_ref):
        def rows_of(i, _):
            at = pl.ds(pl.multiple_of(i * 256, 256), 256)
            mixed = dot(g_ref[at, :], w[l, 2, :, 2 * LOCAL :])
            for h in range(3):
                gm[h, at, :] = mixed[:, LOCAL + HD * h : LOCAL + HD * h + HD].astype(BF)
            for n in range(3):
                lanes = slice(256 * n, 256 * n + 256)
                grad = dot(g_ref[at, :], w[l, 1, :, lanes]) * slope[l, at, lanes]
                gh[at, lanes] = grad.astype(BF)
            return 0

        lax.fori_loop(0, 2, rows_of, 0)

    def back_attend(l):
        for j in (3, 2, 1, 0):
            rows = slice(128 * j, 128 * j + 128)
            seen = slice(0, 128 * j + 128)
            for h in range(3):
                share = probs[l, h, :, stored[j]]
                grad = dot_nt(gm[h, rows, :], v[l, h, seen, :])
                dots = jnp.sum(share * grad, axis=-1, keepdims=True)
                grad = (share * (grad - dots)).astype(BF)
                lanes = slice(HD * h, HD * h + HD)
                key_lanes = slice(LOCAL + HD * h, LOCAL + HD * h + HD)
                dqk[rows, lanes] = dot(grad, k[l, h, seen, :]) * (1.0 / 8.0)
                by_key = dot_tn(grad, q[l, h, rows, :])
                by_value = dot_tn(share.astype(BF), gm[h, rows, :])
                if j == 3:
                    dqk[seen, key_lanes] = by_key
                    dv[seen, lanes] = by_value
                else:
                    dqk[seen, key_lanes] += by_key
                    dv[seen, lanes] += by_value

        def rows_of(i, _):
            at = pl.ds(pl.multiple_of(i * 128, 128), 128)
            gpre[at, 0 : 2 * LOCAL] = turn(dqk[at, :], at, -1).astype(BF)
            gpre[at, 2 * LOCAL :] = jnp.concatenate(
                [dv[at, :], jnp.zeros((128, LOCAL), F32)], axis=1
            ).astype(BF)
            return 0

        lax.fori_loop(0, 4, rows_of, 0)

    def back_norms(l, i, emit):
        rows = slice(256 * i, 256 * i + 256)
        one = dot_nt(gpre[rows, :], w[l, 2])
        two = dot_nt(gh[rows, :], w[l, 0])
        unit = normal[l, rows, :]
        sums = [col_sum(one * unit), col_sum(two * unit), col_sum(one), col_sum(two)]
        for n, value in enumerate(sums):
            row = slice(8 + 4 * l + n, 9 + 4 * l + n)
            vec[row, :] = value if i == 0 else vec[row, :] + value
        mixture = one * vecs[l, 3:4, :] + two * vecs[l, 4:5, :]
        first = jnp.mean(mixture, axis=-1, keepdims=True)
        second = jnp.mean(mixture * unit, axis=-1, keepdims=True)
        part = rstd[l, rows, 0:1] * (mixture - first - unit * second)
        emit(i, slice(0, D), part)

    def sums_of(l, g_ref):
        for n, ref in enumerate((gpre, gh, g_ref)):
            row = slice(4 * l + n, 4 * l + n + 1)
            vec[row, :] = col_sum(ref[...].astype(F32))
        vec[4 * l + 3 : 4 * l + 4, :] = jnp.zeros((1, D), F32)

    def weights_of(l, ch, g_ref):
        def rows_of(m, _):
            lanes = pl.ds(pl.multiple_of(m * 384, 128), 384)
            if ch == 0:
                value = dot_tn(nb[l, :, lanes], gh[...])
            elif ch == 1:
                value = dot_tn(g_ref[:, lanes], act[l])
            else:
                value = dot_tn(na[l, :, lanes], gpre[...])
                other = dot_tn(g_ref[:, lanes], mixp[l])
                value = jnp.concatenate(
                    [value[:, 0 : 2 * LOCAL], value[:, 2 * LOCAL :] + other], axis=1
                )
            grads[ch, pl.ds(4 * m, 4)] = value.astype(BF).reshape(4, 2, 48, D)
            return 0

        lax.fori_loop(0, 2, rows_of, 0)
        cp.start(("rc", l, ch), grads.at[ch, :, 1 - c], sib.at[l, ch], to_c)

    def weights_gone(l, ch):
        cp.sent_off(("rc", l, ch), grads.at[ch, :, 1 - c], sib.at[l, ch], to_c)

    def reduce_core(l, ch):
        cp.landed(("rc", l, ch), sib.at[l, ch])

        def add(i, _):
            sib[l, ch, i] = (sib[l, ch, i].astype(F32) + grads[ch, i, c].astype(F32)).astype(BF)
            return 0

        lax.fori_loop(0, 8, add, 0)
        if ch < 2:
            for j in (1, 3, 2, 0):
                yy = (y + j) % 4
                cp.start(("rx", l, ch, j), sib.at[l, ch, yy * 2 + 1 - x], xbuf.at[l, ch, yy], to_x)
        else:
            for j in (1, 3, 2):
                yy = (y + j) % 4
                cp.start(
                    ("ry", l, ch, j),
                    sib.at[l, ch, pl.ds(yy * 2, 2)],
                    ybuf.at[l, pl.ds(2 * (j - 1), 2)],
                    to_y[j],
                )

    def reduce_mid(l, ch):
        if ch < 2:
            for j in (1, 3, 2, 0):
                yy = (y + j) % 4
                cp.landed(("rx", l, ch, j), xbuf.at[l, ch, yy])
                mine = yy * 2 + x
                xbuf[l, ch, yy] = (
                    sib[l, ch, mine].astype(F32) + xbuf[l, ch, yy].astype(F32)
                ).astype(BF)
                if j:
                    cp.start(
                        ("ry", l, ch, j),
                        xbuf.at[l, ch, yy],
                        ybuf.at[l, 6 + ch * 3 + j - 1],
                        to_y[j],
                    )
        else:
            for j in (1, 3, 2):
                cp.landed(("ry", l, ch, j), ybuf.at[l, pl.ds(2 * (j - 1), 2)])
            for i in range(2):
                total = sib[l, 2, y * 2 + i].astype(F32)
                for j in range(3):
                    total = total + ybuf[l, 2 * j + i].astype(F32)
                keep[l, i] = total.astype(BF)
            cp.start(("rx", l, ch, 0), keep.at[l, 1 - x], keep.at[l, 2], to_x)

    def reduce_end(l, ch):
        if ch < 2:
            total = xbuf[l, ch, y].astype(F32)
            for j in (1, 3, 2):
                cp.landed(("ry", l, ch, j), ybuf.at[l, 6 + ch * 3 + j - 1])
            for j in range(3):
                total = total + ybuf[l, 6 + ch * 3 + j].astype(F32)
        else:
            cp.landed(("rx", l, ch, 0), keep.at[l, 2])
            total = keep[l, x].astype(F32) + keep[l, 2].astype(F32)
        sbuf[l, ch] = total.astype(BF)

        @pl.when(s == 1 - l)
        def _():
            cp.make(("rs", ch), sbuf.at[l, ch], sbuf_in.at[ch], to_s).start()

    @pl.when(s == 1)
    def _():
        swapped()

    gather_first(0)
    prepare()
    fetch_x.wait()
    gather_second(0)

    @pl.when(s == 0)
    def _():
        swapped()

    norms(0, x0)
    gather_third(0)
    gather_first(1)
    gather_fourth(0, (2,))
    attend(0)
    gather_second(1)
    gather_fourth(0, (0, 1))
    feed(0)
    result_rows(0, 0, emit_row(0))
    row_push(0, 0)
    result_rows(0, 1, emit_row(0))
    row_push(0, 1)
    gather_third(1)
    row_finish(0, x0, 0, x1)
    gather_fourth(1)
    fetch_g.wait()
    row_wait(0, x1)

    pack(x1, acts.at[0, 0])
    act_push(0, 0)
    norms(1, x1)
    attend(1)
    feed(1)
    result_rows(1, 0, emit_full)
    result_rows(1, 1, emit_full)
    col_push(0)

    back_heads(1, g1)
    back_attend(1)
    back_norms(1, 0, emit_row(1))
    row_push(1, 0)
    back_norms(1, 1, emit_row(1))
    row_push(1, 1)
    weights_of(1, 1, g1)
    weights_of(1, 0, g1)
    row_finish(1, g1, None, g0)
    weights_of(1, 2, g1)
    sums_of(1, g1)
    for b in range(4):

        @pl.when(t == b)
        def _():
            for i in range(2):
                stage[4, 0:1, LOCAL * i : LOCAL * i + LOCAL] = vecs[
                    1, 2:3, LOCAL * b : LOCAL * b + LOCAL
                ]

    col_finish(0, acts.at[0, 0], True, acts.at[1, 0])
    act_push(1, 0)
    reduce_core(1, 1)
    reduce_core(1, 0)
    reduce_core(1, 2)
    row_wait(1, g0)

    for ch in range(3):
        weights_gone(1, ch)
    pack(g0, acts.at[1, 1])
    act_push(1, 1)
    back_heads(0, g0)
    reduce_mid(1, 1)
    reduce_mid(1, 0)
    reduce_mid(1, 2)
    weights_of(0, 1, g0)
    weights_of(0, 0, g0)
    back_attend(0)
    for ch in (1, 0, 2):
        reduce_end(1, ch)
    back_norms(0, 0, emit_full)
    back_norms(0, 1, emit_full)
    col_push(1)
    sums_of(0, g0)
    vland[t, 0:8] = vec[8:16, :]
    for j in (1, 2, 3):
        cp.start(("vz", j), vec.at[pl.ds(8, 8)], vland.at[t, pl.ds(0, 8)], to_z[j])
    weights_of(0, 2, g0)
    reduce_core(0, 1)
    reduce_core(0, 0)
    for j in (1, 2, 3):
        cp.landed(("vz", j), vland.at[(t + 4 - j) % 4, pl.ds(0, 8)])
    stage[0, 0:8] = vec[0:8, :]
    stage[0, 8:16] = vland[0, 0:8] + vland[1, 0:8] + vland[2, 0:8] + vland[3, 0:8]
    cp.start("vc", stage.at[0], vland.at[4], to_c)
    reduce_core(0, 2)
    cp.landed("vc", vland.at[4])
    stage[1] = stage[0] + vland[4]
    cp.start("vx", stage.at[1], vland.at[5], to_x)
    reduce_mid(0, 1)
    reduce_mid(0, 0)
    cp.landed("vx", vland.at[5])
    stage[2] = stage[1] + vland[5]
    cp.start("vs", stage.at[2], vland.at[6], to_s)
    col_finish(1, acts.at[1, 1], False, acts.at[0, 1])
    act_push(0, 1)
    reduce_mid(0, 2)
    cp.landed("vs", vland.at[6])
    stage[3] = stage[2] + vland[6]
    vland[7 + y] = stage[3]
    for j in (1, 2, 3):
        cp.start(("vy", j), stage.at[3], vland.at[7 + y], to_y[j])
    for ch in (1, 0, 2):
        reduce_end(0, ch)

    def unpack(out, ref, m):
        out[m, 0:256, :] = ref[:, 0:LOCAL]
        out[m, 256:512, :] = ref[:, LOCAL : 2 * LOCAL]

    unpack(sec_out, acts.at[s, 0], s)
    unpack(grad_out, acts.at[s, 1], s)
    cp.landed(("act", 0), acts_in.at[0])
    unpack(sec_out, acts_in.at[0], 1 - s)
    cp.landed(("act", 1), acts_in.at[1])
    unpack(grad_out, acts_in.at[1], 1 - s)
    for j in (1, 2, 3):
        cp.landed(("vy", j), vland.at[7 + (y + 4 - j) % 4])
    stage[4] = vland[7] + vland[8] + vland[9] + vland[10]
    va_out[...] = stage[4, 0:8]
    vb_out[...] = stage[4, 8:16]
    for ch in (1, 0, 2):
        cp.landed(("rs", ch), sbuf_in.at[ch])
        w_out[ch] = sbuf[s, ch].astype(F32) + sbuf_in[ch].astype(F32)
        name = ("rs", ch)
        cp.late(name, cp.make(name, sbuf.at[1 - s, ch], sbuf_in.at[ch], to_s))
    for kind in range(2):
        name = ("act", kind)
        cp.late(name, cp.make(name, acts.at[1 - s, kind], acts_in.at[kind], to_s))
    cp.finish()


def mega(*arguments):
    dma = pltpu.SemaphoreType.DMA
    vmem = pl.BlockSpec(memory_space=pltpu.VMEM)
    smem = pl.BlockSpec(memory_space=pltpu.SMEM)
    anywhere = pl.BlockSpec(memory_space=pl.ANY)

    def bf(*shape):
        return pltpu.VMEM(shape, BF)

    def f32(*shape):
        return pltpu.VMEM(shape, F32)

    return pl.pallas_call(
        mega_kernel,
        out_shape=[
            jax.ShapeDtypeStruct((2, SLOT, LOCAL), BF),
            jax.ShapeDtypeStruct((2, SLOT, LOCAL), BF),
            jax.ShapeDtypeStruct((3, 48, D), F32),
            jax.ShapeDtypeStruct((8, D), F32),
            jax.ShapeDtypeStruct((8, D), F32),
        ],
        in_specs=[smem, vmem, anywhere, anywhere] + [vmem] * 9,
        out_specs=[vmem] * 5,
        scratch_shapes=[
            bf(2, 3, D, D),
            f32(2, 8, D),
            bf(SLOT, D),
            bf(SLOT, D),
            bf(SLOT, D),
            bf(SLOT, D),
            f32(3, SLOT, 128),
            f32(SLOT, SLOT),
            f32(2, SLOT, D),
            f32(2, SLOT, 128),
            bf(2, SLOT, D),
            bf(2, SLOT, D),
            bf(2, 3, SLOT, HD),
            bf(2, 3, SLOT, HD),
            bf(2, 3, SLOT, HD),
            f32(2, 3, 128, 1280),
            bf(2, SLOT, 2 * LOCAL),
            bf(2, SLOT, D),
            f32(2, SLOT, D),
            bf(3, SLOT, HD),
            bf(SLOT, D),
            f32(SLOT, 2 * LOCAL),
            f32(SLOT, LOCAL),
            bf(SLOT, D),
            bf(SLOT, D),
            bf(2, 4, 128, D),
            bf(2, 4, 256, 2 * LOCAL),
            bf(2, 3, 128, D),
            bf(2, 3, 256, 2 * LOCAL),
            bf(2, 2, 256, 2 * LOCAL),
            bf(2, 256, 2 * LOCAL),
            bf(3, 8, 2, 48, D),
            bf(2, 3, 8, 48, D),
            bf(2, 2, 4, 48, D),
            bf(2, 12, 48, D),
            bf(2, 3, 48, D),
            bf(2, 3, 48, D),
            bf(3, 48, D),
            f32(16, D),
            f32(11, 16, D),
            f32(5, 16, D),
            dma((SEMS,)),
            dma((SEMS,)),
            dma((2,)),
        ],
        compiler_params=pltpu.CompilerParams(
            collective_id=0, has_side_effects=True, vmem_limit_bytes=VMEM_LIMIT
        ),
        name="two_layers",
    )(*arguments)


def body(
    inputs,
    cotangent,
    seq_lengths,
    w_qkv,
    b_qkv,
    w_attn_out,
    w_in,
    b_in,
    w_out,
    b_out,
    norm_gains,
    norm_biases,
):
    s = lax.axis_index("section")
    powers = 1.0 / 10000.0 ** (np.arange(ROT // 2, dtype=np.float32) * 2.0 / ROT)
    freq = jnp.asarray(np.tile(powers.astype(np.float32), 128 // (ROT // 2))[None])
    qkv_bias = jnp.pad(b_qkv.reshape(1, -1), ((0, 0), (0, LOCAL)))
    sec, grad, w_sums, va, vb = mega(
        seq_lengths[:, 0],
        freq,
        inputs,
        cotangent,
        w_qkv[0].reshape(48, 3 * LOCAL),
        w_attn_out[0],
        w_in[0],
        w_out[0],
        qkv_bias,
        b_in,
        b_out,
        norm_gains[0],
        norm_biases[0],
    )
    va = lax.dynamic_slice_in_dim(va, s * 4, 4, 0)
    vb = lax.dynamic_slice_in_dim(vb, s * 4, 4, 0)
    return (
        sec[None],
        grad[None],
        w_sums[2, :, : 3 * LOCAL].reshape(1, 48, 3, LOCAL),
        va[0, : 3 * LOCAL].reshape(1, 3, LOCAL),
        w_sums[2, :, 3 * LOCAL :].T[None],
        w_sums[0][None],
        va[1][None],
        w_sums[1].T[None],
        va[2][None],
        vb[0:2][None],
        vb[2:4][None],
    )


def solution(mesh):
    return jax.shard_map(
        body,
        mesh=mesh,
        in_specs=(
            P(None, "dp", None),
            P(None, "dp", None),
            P(None, "dp", None),
            P("section", "dp", None, "tensor"),
            P("section", None, "tensor"),
            P("section", "tensor", "dp"),
            P("section", "dp", "tensor"),
            P("section", "tensor"),
            P("section", "tensor", "dp"),
            P("section", None),
            P("section", None, None),
            P("section", None, None),
        ),
        out_specs=(
            P("section", None, "dp", "tensor"),
            P("section", None, "dp", "tensor"),
            P("section", "dp", None, "tensor"),
            P("section", None, "tensor"),
            P("section", "tensor", "dp"),
            P("section", "dp", "tensor"),
            P("section", "tensor"),
            P("section", "tensor", "dp"),
            P("section", None),
            P("section", None, None),
            P("section", None, None),
        ),
        check_vma=False,
    )
```

```python
import math

import jax
import jax.numpy as jnp
import numpy as np
from jax import lax
from jax.experimental import pallas as pl
from jax.experimental.pallas import tpu as pltpu
from jax.sharding import PartitionSpec as P

HD = 64
ROT = 16
BLOCK = 128
SEQS = 4
SLOT = 512
D = 768
LOCAL = 192
EPSILON = 1e-05
MASKED = -1e30
MESH = pl.DeviceIdType.MESH
BF = jnp.bfloat16
F32 = jnp.float32
VMEM_LIMIT = 58 * 2**20


def coords():
    dp = lax.axis_index("dp")
    return (
        lax.axis_index("section"),
        dp // 4,
        (dp // 2) % 2,
        dp % 2,
        lax.axis_index("tensor"),
    )


def dp_of(y, x, c):
    return y * 4 + x * 2 + c


def signal_all(targets):
    barrier = pltpu.get_barrier_semaphore()
    for target in targets:
        pl.semaphore_signal(barrier, inc=1, device_id=target, device_id_type=MESH)
    pl.semaphore_wait(barrier, len(targets))


def remote(src, dst, send, recv, target):
    return pltpu.make_async_remote_copy(
        src_ref=src,
        dst_ref=dst,
        send_sem=send,
        recv_sem=recv,
        device_id=target,
        device_id_type=MESH,
    )


def dot(a, b):
    return lax.dot_general(a, b, (((1,), (0,)), ((), ())), preferred_element_type=F32)


def dot_nt(a, b):
    return lax.dot_general(a, b, (((1,), (1,)), ((), ())), preferred_element_type=F32)


def dot_tn(a, b):
    return lax.dot_general(a, b, (((0,), (0,)), ((), ())), preferred_element_type=F32)


def gelu_parts(h):
    tail = 1.0 / (1.0 + (0.3275911 / math.sqrt(2.0)) * jnp.abs(h))
    bell = jnp.exp(h * h * -0.5)
    series = 0.5 * 1.061405429
    for term in (-1.453152027, 1.421413741, -0.284496736, 0.254829592):
        series = series * tail + 0.5 * term
    below = series * tail * bell
    phi = jnp.where(h >= 0.0, 1.0 - below, below)
    return h * phi, phi + h * bell * (1.0 / math.sqrt(2.0 * math.pi))


def col_sum(values):
    return jnp.sum(values, axis=0, keepdims=True)


class Copies:
    def __init__(self, send, recv, to_any):
        self.send, self.recv, self.to_any = send, recv, to_any
        self.numbers = {}
        self.sent = []
        self.done = set()

    def make(self, name, src, dst, to):
        number = self.numbers.setdefault(name, len(self.numbers))
        assert number < SEMS
        return remote(src, dst, self.send.at[number], self.recv.at[number], to)

    def start(self, name, src, dst, to):
        copy = self.make(name, src, dst, to)
        copy.start()
        self.late(name, copy)

    def late(self, name, copy):
        self.sent.append((self.numbers[name], copy))

    def landed(self, name, ref):
        self.make(name, ref, ref, self.to_any).wait_recv()

    def sent_off(self, name, src, dst, to):
        copy = self.make(name, src, dst, to)
        copy.wait_send()
        self.done.add(self.numbers[name])

    def finish(self):
        for number, copy in self.sent:
            if number not in self.done:
                copy.wait_send()


SEMS = 240


def mega_kernel(
    len_ref,
    freq_ref,
    inputs_ref,
    cot_ref,
    wqkv_ref,
    wattn_ref,
    win_ref,
    wout_ref,
    bqkv_ref,
    bin_ref,
    bout_ref,
    gains_ref,
    shifts_ref,
    acts_out,
    w_out,
    vec_out,
    w,
    vecs,
    x0,
    x1,
    g1,
    g0,
    tables,
    bias,
    normal,
    rstd,
    na,
    nb,
    q,
    k,
    v,
    probs,
    mixp,
    act,
    slope,
    gm,
    gh,
    dqk,
    dv,
    gpre,
    full,
    zrow,
    zcol,
    zland,
    zland_c,
    acts,
    acts_in,
    grads,
    sib,
    xbuf,
    ybuf,
    keep,
    sbuf,
    sbuf_in,
    vec,
    vland,
    stage,
    send,
    recv,
    local,
):
    s, y, x, c, t = coords()
    me = dp_of(y, x, c)
    to_y = {j: {"dp": dp_of((y + j) % 4, x, c)} for j in (1, 2, 3)}
    to_z = {j: {"tensor": (t + j) % 4} for j in (1, 2, 3)}
    to_x = {"dp": dp_of(y, 1 - x, c)}
    to_c = {"dp": dp_of(y, x, 1 - c)}
    to_s = {"section": 1 - s}
    cp = Copies(send, recv, to_c)

    fetch_x = pltpu.make_async_copy(inputs_ref.at[s], x0, local.at[0])
    fetch_g = pltpu.make_async_copy(cot_ref.at[s], g1, local.at[1])
    fetch_x.start()
    fetch_g.start()

    def rows48(block):
        return pl.ds(pl.multiple_of(block * 48, 16), 48)

    w[s, 0, rows48(me), :] = win_ref[...]
    w[s, 1, rows48(me), :] = wout_ref[...]
    w[s, 2, rows48(me), :] = jnp.concatenate(
        [wqkv_ref[0], wqkv_ref[1], wqkv_ref[2], wattn_ref[...]], axis=1
    )
    vecs[s, 0:1, :] = jnp.concatenate(
        [bqkv_ref[0], bqkv_ref[1], bqkv_ref[2], jnp.zeros((1, LOCAL), F32)], axis=1
    )
    vecs[s, 1:2, :] = bin_ref[...]
    vecs[s, 2:3, :] = bout_ref[...]
    vecs[s, 3:5, :] = gains_ref[...]
    vecs[s, 5:7, :] = shifts_ref[...]
    vecs[s, 7:8, :] = jnp.zeros((1, D), F32)

    signal_all(list(to_y.values()) + list(to_z.values()) + [to_x, to_c, to_s])

    cp.start("swap_w", w.at[s, :, rows48(me)], w.at[s, :, rows48(me)], to_s)
    cp.start("swap_v", vecs.at[s], vecs.at[s], to_s)

    def swapped():
        cp.landed("swap_w", w.at[1 - s, :, rows48(me)])
        cp.landed("swap_v", vecs.at[1 - s])

    def block_of(j, other, core=c):
        return dp_of((y + 4 - j) % 4, (1 - x) if other else x, core)

    def push(l, ch, slot, block, to):
        ref = w.at[l, ch, rows48(block)]
        cp.start(("w", l, ch, slot), ref, ref, to)

    def arrived(l, ch, slot, block):
        cp.landed(("w", l, ch, slot), w.at[l, ch, rows48(block)])

    def gather_first(l, ch):
        if ch == 1:
            for j in (1, 3, 2):
                push(l, ch, j - 1, me, to_y[j])
            push(l, ch, 3, me, to_x)
        else:
            push(l, ch, 0, me, to_x)
            for j in (1, 3, 2):
                push(l, ch, j, me, to_y[j])
        push(l, ch, 7, me, to_c)

    def gather_second(l, ch):
        if ch == 1:
            for j in (1, 3, 2):
                arrived(l, ch, j - 1, block_of(j, False))
                push(l, ch, 3 + j, block_of(j, False), to_x)
                push(l, ch, 7 + 2 * j, block_of(j, False), to_c)
        else:
            arrived(l, ch, 0, block_of(0, True))
            for j in (1, 3, 2):
                push(l, ch, 3 + j, block_of(0, True), to_y[j])
            push(l, ch, 8, block_of(0, True), to_c)

    def gather_third(l, ch):
        if ch == 1:
            for j in (0, 1, 3, 2):
                arrived(l, ch, 3 + j, block_of(j, True))
                push(l, ch, 8 + 2 * j, block_of(j, True), to_c)
        else:
            for j in (1, 3, 2):
                arrived(l, ch, j, block_of(j, False))
                push(l, ch, 7 + 2 * j, block_of(j, False), to_c)
            for j in (1, 3, 2):
                arrived(l, ch, 3 + j, block_of(j, True))
                push(l, ch, 8 + 2 * j, block_of(j, True), to_c)

    def gather_fourth(l, ch):
        for j in range(4):
            arrived(l, ch, 7 + 2 * j, block_of(j, False, 1 - c))
            arrived(l, ch, 8 + 2 * j, block_of(j, True, 1 - c))

    def prepare():
        lens = [len_ref[s, j] for j in range(SEQS)]
        ends, total = [], 0
        for j in range(SEQS):
            total = total + ((lens[j] + (BLOCK - 1)) >> 7)
            ends.append(total)

        def rows_of(i, _):
            at = pl.ds(pl.multiple_of(i * 128, 128), 128)
            row = i * 128 + lax.broadcasted_iota(jnp.int32, (128, SLOT), 0)
            col = lax.broadcasted_iota(jnp.int32, (128, SLOT), 1)
            block = i
            begin = jnp.int32(0)
            owner = jnp.int32(0)
            for j in range(SEQS):
                past = (ends[j] <= block).astype(jnp.int32)
                begin = jnp.maximum(begin, past * ends[j])
                owner = owner + past
            begin = begin * BLOCK
            size = jnp.int32(0)
            for j in range(SEQS):
                size = size + (owner == j).astype(jnp.int32) * lens[j]
            fine = (col >= begin) & (col <= row) & (col < begin + size) | (col == row)
            bias[at, :] = jnp.where(fine, 0.0, MASKED)
            offset = (row[:, :128] - begin).astype(F32)
            angles = offset * freq_ref[...]
            lane = lax.broadcasted_iota(jnp.int32, (128, 128), 1) & 63
            cosines, sines = jnp.cos(angles), jnp.sin(angles)
            tables[0, at, :] = jnp.where(lane < ROT, cosines, 1.0)
            tables[1, at, :] = jnp.where(lane < ROT // 2, -sines, 0.0)
            tables[2, at, :] = jnp.where((lane >= ROT // 2) & (lane < ROT), sines, 0.0)
            return 0

        lax.fori_loop(0, 4, rows_of, 0)

    def turn(values, at, sign):
        ahead = pltpu.roll(values, 384 - ROT // 2, 1)
        behind = pltpu.roll(values, ROT // 2, 1)
        parts = []
        for b in range(3):
            lanes = slice(128 * b, 128 * b + 128)
            change = ahead[:, lanes] * tables[1, at, :] + behind[:, lanes] * tables[2, at, :]
            base = values[:, lanes] * tables[0, at, :]
            parts.append(base + change if sign > 0 else base - change)
        return jnp.concatenate(parts, axis=1)

    def norms(l, x_ref, half):
        def rows_of(i, _):
            at = pl.ds(pl.multiple_of(256 * half + i * 64, 64), 64)
            values = x_ref[at, :].astype(F32)
            centred = values - jnp.mean(values, axis=-1, keepdims=True)
            scale = lax.rsqrt(jnp.mean(centred * centred, axis=-1, keepdims=True) + EPSILON)
            unit = centred * scale
            normal[l, at, :] = unit
            rstd[l, at, :] = jnp.broadcast_to(scale, (64, 128))
            na[l, at, :] = (unit * vecs[l, 3:4, :] + vecs[l, 5:6, :]).astype(BF)
            nb[l, at, :] = (unit * vecs[l, 4:5, :] + vecs[l, 6:7, :]).astype(BF)
            return 0

        lax.fori_loop(0, 4, rows_of, 0)

    stored = [slice(64 * j * (j + 1), 64 * (j + 1) * (j + 2)) for j in range(4)]

    def project(l, half):
        at = slice(256 * half, 256 * half + 256)
        pre = dot(na[l, at, :], w[l, 2, :, 0 : 3 * LOCAL]) + vecs[l, 0:1, 0 : 3 * LOCAL]
        turned = turn(pre[:, 0 : 2 * LOCAL], at, 1)
        for h in range(3):
            q[l, h, at, :] = (turned[:, HD * h : HD * h + HD] * (1.0 / 8.0)).astype(BF)
            k[l, h, at, :] = turned[:, LOCAL + HD * h : LOCAL + HD * h + HD].astype(BF)
            v[l, h, at, :] = pre[:, 2 * LOCAL + HD * h : 2 * LOCAL + HD * h + HD].astype(BF)
        mixp[l, at, 0:LOCAL] = jnp.zeros((256, LOCAL), BF)

    def attend(l, j):
        rows = slice(128 * j, 128 * j + 128)
        seen = slice(0, 128 * j + 128)
        for h in range(3):
            scores = dot_nt(q[l, h, rows, :], k[l, h, seen, :]) + bias[rows, seen]
            weights = jnp.exp(scores - jnp.max(scores, axis=-1, keepdims=True))
            share = weights * (1.0 / jnp.sum(weights, axis=-1, keepdims=True))
            probs[l, h, :, stored[j]] = share
            out = dot(share.astype(BF), v[l, h, seen, :])
            mixp[l, rows, LOCAL + HD * h : LOCAL + HD * h + HD] = out.astype(BF)

    def feed(l, half):
        at = slice(256 * half, 256 * half + 256)
        for n in range(3):
            lanes = slice(256 * n, 256 * n + 256)
            hidden = dot(nb[l, at, :], w[l, 0, :, lanes]) + vecs[l, 1:2, lanes]
            value, grade = gelu_parts(hidden)
            act[l, at, lanes] = value.astype(BF)
            slope[l, at, lanes] = grade

    def result_rows(l, i, emit):
        rows = slice(256 * i, 256 * i + 256)
        for n in range(3):
            lanes = slice(256 * n, 256 * n + 256)
            part = dot_nt(act[l, rows, :], w[l, 1, lanes, :])
            part = part + dot_nt(mixp[l, rows, :], w[l, 2, lanes, 2 * LOCAL :])
            emit(i, lanes, part)

    def emit_row(use):
        def emit(i, lanes, part):
            for b in range(4):
                zrow[use, i, b, :, lanes] = part[64 * b : 64 * b + 64].astype(BF)

        return emit

    def emit_full(i, lanes, part):
        full[256 * i : 256 * i + 256, lanes] = part.astype(BF)

    def shared(i, b):
        return pl.ds(pl.multiple_of(256 * i + b * 64, 64), 64)

    def row_push(use, i):
        for j in (1, 3, 2):
            cp.start(
                ("zr", use, i, j), zrow.at[use, i, (t + j) % 4], zland.at[use, i, j - 1], to_z[j]
            )

    def row_finish(use, i, extra, with_bias, out_ref):
        for j in (1, 3, 2):
            cp.landed(("zr", use, i, j), zland.at[use, i, j - 1])
        here = shared(i, t)
        total = extra[here, :].astype(F32) + zrow[use, i, t].astype(F32)
        if with_bias is not None:
            total = total + vecs[with_bias, 2:3, :]
        for j in range(3):
            total = total + zland[use, i, j].astype(F32)
        out_ref[here, :] = total.astype(BF)
        for j in (1, 3, 2):
            cp.start(("za", use, i, j), out_ref.at[here], out_ref.at[here], to_z[j])

    def row_wait(use, i, out_ref):
        for j in (1, 3, 2):
            cp.landed(("za", use, i, j), out_ref.at[shared(i, (t + 4 - j) % 4)])

    def chosen(b):
        row = lax.broadcasted_iota(jnp.int32, (LOCAL, D), 0)
        return lax.broadcasted_iota(jnp.int32, (LOCAL, D), 1) == row + b * LOCAL

    def pack(ref, out):
        out[...] = dot_nt(chosen(t).astype(BF), ref[...]).astype(BF)

    def result_cols(l, use):
        for b in range(4):
            rows = slice(LOCAL * b, LOCAL * b + LOCAL)
            part = dot_nt(w[l, 1, rows, :], act[l])
            part = part + dot_nt(w[l, 2, rows, 2 * LOCAL :], mixp[l])
            zcol[use, b] = part.astype(BF)

    def half_of(i):
        return slice(256 * i, 256 * i + 256)

    def turn_cols(use, i):
        for b in range(4):
            zcol[use, b, :, half_of(i)] = dot_nt(
                chosen(b).astype(BF), full[half_of(i), :]
            ).astype(BF)

    def col_push(use, i):
        for j in (1, 3, 2):
            cp.start(
                ("zc", use, i, j),
                zcol.at[use, (t + j) % 4, :, half_of(i)],
                zland_c.at[use, j - 1, :, half_of(i)],
                to_z[j],
            )

    def col_finish(use, i, extra, with_bias, l, kind):
        lanes = half_of(i)
        for j in (1, 3, 2):
            cp.landed(("zc", use, i, j), zland_c.at[use, j - 1, :, lanes])
        total = extra[:, lanes].astype(F32) + zcol[use, t, :, lanes].astype(F32)
        if with_bias is not None:
            total = total + jnp.sum(
                jnp.where(chosen(t), vecs[with_bias, 2:3, :], 0.0), axis=1, keepdims=True
            )
        for j in range(3):
            total = total + zland_c[use, j, :, lanes].astype(F32)
        acts[l, kind, :, lanes] = total.astype(BF)
        act_push(l, kind, i)

    def act_copy(l, kind, i):
        ref = acts.at[l, kind, :, half_of(i)]
        return cp.make(("act", kind, i), ref, acts_in.at[kind, :, half_of(i)], to_s)

    def act_push(l, kind, i):
        @pl.when(s == 1 - l)
        def _():
            act_copy(l, kind, i).start()

    def back_heads(l, g_ref, half):
        at = slice(256 * half, 256 * half + 256)
        mixed = dot(g_ref[at, :], w[l, 2, :, 2 * LOCAL :])
        for h in range(3):
            gm[h, at, :] = mixed[:, LOCAL + HD * h : LOCAL + HD * h + HD].astype(BF)
        for n in range(3):
            lanes = slice(256 * n, 256 * n + 256)
            grad = dot(g_ref[at, :], w[l, 1, :, lanes]) * slope[l, at, lanes]
            gh[at, lanes] = grad.astype(BF)

    def back_attend(l, j):
        rows = slice(128 * j, 128 * j + 128)
        seen = slice(0, 128 * j + 128)
        for h in range(3):
            share = probs[l, h, :, stored[j]]
            grad = dot_nt(gm[h, rows, :], v[l, h, seen, :])
            dots = jnp.sum(share * grad, axis=-1, keepdims=True)
            grad = (share * (grad - dots)).astype(BF)
            lanes = slice(HD * h, HD * h + HD)
            key_lanes = slice(LOCAL + HD * h, LOCAL + HD * h + HD)
            dqk[rows, lanes] = dot(grad, k[l, h, seen, :]) * (1.0 / 8.0)
            by_key = dot_tn(grad, q[l, h, rows, :])
            by_value = dot_tn(share.astype(BF), gm[h, rows, :])
            if j == 3:
                dqk[seen, key_lanes] = by_key
                dv[seen, lanes] = by_value
            else:
                dqk[seen, key_lanes] += by_key
                dv[seen, lanes] += by_value

    def back_turn():
        def rows_of(i, _):
            at = pl.ds(pl.multiple_of(i * 128, 128), 128)
            gpre[at, 0 : 2 * LOCAL] = turn(dqk[at, :], at, -1).astype(BF)
            gpre[at, 2 * LOCAL :] = jnp.concatenate(
                [dv[at, :], jnp.zeros((128, LOCAL), F32)], axis=1
            ).astype(BF)
            return 0

        lax.fori_loop(0, 4, rows_of, 0)

    def back_norms(l, i, emit):
        rows = slice(256 * i, 256 * i + 256)
        one = dot_nt(gpre[rows, :], w[l, 2])
        two = dot_nt(gh[rows, :], w[l, 0])
        unit = normal[l, rows, :]
        sums = [col_sum(one * unit), col_sum(two * unit), col_sum(one), col_sum(two)]
        for n, value in enumerate(sums):
            row = slice(8 + 4 * l + n, 9 + 4 * l + n)
            vec[row, :] = value if i == 0 else vec[row, :] + value
        mixture = one * vecs[l, 3:4, :] + two * vecs[l, 4:5, :]
        first = jnp.mean(mixture, axis=-1, keepdims=True)
        second = jnp.mean(mixture * unit, axis=-1, keepdims=True)
        part = rstd[l, rows, 0:1] * (mixture - first - unit * second)
        emit(i, slice(0, D), part)

    def sums_of(l, g_ref):
        for n, ref in enumerate((gpre, gh, g_ref)):
            row = slice(4 * l + n, 4 * l + n + 1)
            vec[row, :] = col_sum(ref[...].astype(F32))
        vec[4 * l + 3 : 4 * l + 4, :] = jnp.zeros((1, D), F32)

    def weights_of(l, ch, g_ref):
        def rows_of(m, _):
            lanes = pl.ds(pl.multiple_of(m * 384, 128), 384)
            if ch == 0:
                value = dot_tn(nb[l, :, lanes], gh[...])
            elif ch == 1:
                value = dot_tn(g_ref[:, lanes], act[l])
            else:
                value = dot_tn(na[l, :, lanes], gpre[...])
                other = dot_tn(g_ref[:, lanes], mixp[l])
                value = jnp.concatenate(
                    [value[:, 0 : 2 * LOCAL], value[:, 2 * LOCAL :] + other], axis=1
                )
            grads[ch, pl.ds(4 * m, 4)] = value.astype(BF).reshape(4, 2, 48, D)
            return 0

        lax.fori_loop(0, 2, rows_of, 0)
        cp.start(("rc", l, ch), grads.at[ch, :, 1 - c], sib.at[l, ch], to_c)

    def weights_gone(l, ch):
        cp.sent_off(("rc", l, ch), grads.at[ch, :, 1 - c], sib.at[l, ch], to_c)

    def reduce_core(l, ch):
        cp.landed(("rc", l, ch), sib.at[l, ch])

        def add(i, _):
            sib[l, ch, i] = (sib[l, ch, i].astype(F32) + grads[ch, i, c].astype(F32)).astype(BF)
            return 0

        lax.fori_loop(0, 8, add, 0)
        if ch == 1:
            for j in (1, 3, 2, 0):
                yy = (y + j) % 4
                cp.start(("rx", l, ch, j), sib.at[l, ch, yy * 2 + 1 - x], xbuf.at[l, yy], to_x)
        else:
            for j in (1, 3, 2):
                yy = (y + j) % 4
                cp.start(
                    ("ry", l, ch, j),
                    sib.at[l, ch, pl.ds(yy * 2, 2)],
                    ybuf.at[l, pl.ds(3 * ch + 2 * (j - 1), 2)],
                    to_y[j],
                )

    def reduce_mid(l, ch):
        if ch == 1:
            for j in (1, 3, 2, 0):
                yy = (y + j) % 4
                cp.landed(("rx", l, ch, j), xbuf.at[l, yy])
                mine = yy * 2 + x
                xbuf[l, yy] = (sib[l, ch, mine].astype(F32) + xbuf[l, yy].astype(F32)).astype(BF)
                if j:
                    cp.start(("ry", l, ch, j), xbuf.at[l, yy], ybuf.at[l, 11 + j], to_y[j])
        else:
            for j in (1, 3, 2):
                cp.landed(("ry", l, ch, j), ybuf.at[l, pl.ds(3 * ch + 2 * (j - 1), 2)])
            for i in range(2):
                total = sib[l, ch, y * 2 + i].astype(F32)
                for j in range(3):
                    total = total + ybuf[l, 3 * ch + 2 * j + i].astype(F32)
                keep[l, ch // 2, i] = total.astype(BF)
            cp.start(("rx", l, ch, 0), keep.at[l, ch // 2, 1 - x], keep.at[l, ch // 2, 2], to_x)

    def reduce_end(l, ch):
        if ch == 1:
            total = xbuf[l, y].astype(F32)
            for j in (1, 3, 2):
                cp.landed(("ry", l, ch, j), ybuf.at[l, 11 + j])
            for j in (1, 2, 3):
                total = total + ybuf[l, 11 + j].astype(F32)
        else:
            cp.landed(("rx", l, ch, 0), keep.at[l, ch // 2, 2])
            total = keep[l, ch // 2, x].astype(F32) + keep[l, ch // 2, 2].astype(F32)
        sbuf[l, ch] = total.astype(BF)

        @pl.when(s == 1 - l)
        def _():
            cp.make(("rs", ch), sbuf.at[l, ch], sbuf_in.at[ch], to_s).start()

    def vec_z():
        vland[t, 0:8] = vec[8:16, :]
        for j in (1, 2, 3):
            cp.start(("vz", j), vec.at[pl.ds(8, 8)], vland.at[t, pl.ds(0, 8)], to_z[j])

    def vec_c():
        for j in (1, 2, 3):
            cp.landed(("vz", j), vland.at[(t + 4 - j) % 4, pl.ds(0, 8)])
        stage[0, 0:8] = vec[0:8, :]
        stage[0, 8:16] = vland[0, 0:8] + vland[1, 0:8] + vland[2, 0:8] + vland[3, 0:8]
        cp.start("vc", stage.at[0], vland.at[4], to_c)

    def vec_x():
        cp.landed("vc", vland.at[4])
        stage[1] = stage[0] + vland[4]
        cp.start("vx", stage.at[1], vland.at[5], to_x)

    def vec_s():
        cp.landed("vx", vland.at[5])
        stage[2] = stage[1] + vland[5]
        cp.start("vs", stage.at[2], vland.at[6], to_s)

    def vec_y():
        cp.landed("vs", vland.at[6])
        stage[3] = stage[2] + vland[6]
        vland[7 + y] = stage[3]
        for j in (1, 2, 3):
            cp.start(("vy", j), stage.at[3], vland.at[7 + y], to_y[j])

    @pl.when(s == 1)
    def _():
        swapped()

    gather_first(0, 2)
    prepare()
    gather_second(0, 2)
    gather_first(0, 0)
    gather_first(0, 1)
    fetch_x.wait()
    norms(0, x0, 0)
    gather_second(0, 0)
    norms(0, x0, 1)
    gather_third(0, 2)
    gather_second(0, 1)

    @pl.when(s == 0)
    def _():
        swapped()

    gather_fourth(0, 2)
    project(0, 0)
    project(0, 1)
    attend(0, 0)
    attend(0, 1)
    gather_third(0, 0)
    gather_third(0, 1)
    gather_first(1, 2)
    gather_first(1, 0)
    gather_first(1, 1)
    attend(0, 2)
    attend(0, 3)
    gather_fourth(0, 0)
    feed(0, 0)
    gather_fourth(0, 1)
    result_rows(0, 0, emit_row(0))
    row_push(0, 0)
    gather_second(1, 2)
    gather_second(1, 0)
    feed(0, 1)
    result_rows(0, 1, emit_row(0))
    row_push(0, 1)
    gather_second(1, 1)
    row_finish(0, 0, x0, 0, x1)
    gather_third(1, 2)
    gather_third(1, 0)
    row_finish(0, 1, x0, 0, x1)
    gather_third(1, 1)
    gather_fourth(1, 2)
    row_wait(0, 0, x1)

    norms(1, x1, 0)
    project(1, 0)
    attend(1, 0)
    attend(1, 1)
    row_wait(0, 1, x1)
    norms(1, x1, 1)
    project(1, 1)
    attend(1, 2)
    attend(1, 3)
    gather_fourth(1, 0)
    feed(1, 0)
    feed(1, 1)
    gather_fourth(1, 1)
    result_cols(1, 0)
    col_push(0, 0)
    col_push(0, 1)
    pack(x1, acts.at[0, 0])
    act_push(0, 0, 0)
    act_push(0, 0, 1)

    fetch_g.wait()
    back_heads(1, g1, 0)
    back_heads(1, g1, 1)
    for j in (3, 2, 1, 0):
        back_attend(1, j)
    back_turn()
    back_norms(1, 0, emit_row(1))
    row_push(1, 0)
    back_norms(1, 1, emit_row(1))
    row_push(1, 1)
    weights_of(1, 1, g1)
    weights_of(1, 0, g1)
    row_finish(1, 0, g1, None, g0)
    weights_of(1, 2, g1)
    reduce_core(1, 1)
    row_finish(1, 1, g1, None, g0)
    reduce_core(1, 0)
    sums_of(1, g1)
    reduce_core(1, 2)
    for i in range(2):
        col_finish(0, i, acts.at[0, 0], 1, 1, 0)
    for ch in range(3):
        weights_gone(1, ch)

    row_wait(1, 0, g0)
    back_heads(0, g0, 0)
    row_wait(1, 1, g0)
    back_heads(0, g0, 1)
    weights_of(0, 1, g0)
    weights_of(0, 0, g0)
    reduce_mid(1, 1)
    reduce_mid(1, 0)
    back_attend(0, 3)
    reduce_mid(1, 2)
    reduce_core(0, 1)
    reduce_core(0, 0)
    back_attend(0, 2)
    reduce_end(1, 1)
    reduce_end(1, 0)
    reduce_end(1, 2)
    back_attend(0, 1)
    back_attend(0, 0)
    back_turn()
    back_norms(0, 0, emit_full)
    turn_cols(1, 0)
    col_push(1, 0)
    back_norms(0, 1, emit_full)
    turn_cols(1, 1)
    col_push(1, 1)
    pack(g0, acts.at[1, 1])
    act_push(1, 1, 0)
    act_push(1, 1, 1)
    weights_of(0, 2, g0)
    sums_of(0, g0)
    vec_z()
    reduce_mid(0, 1)
    reduce_core(0, 2)
    vec_c()
    reduce_mid(0, 0)
    vec_x()
    col_finish(1, 0, acts.at[1, 1], None, 0, 1)
    vec_s()
    reduce_end(0, 1)
    reduce_end(0, 0)
    reduce_mid(0, 2)
    col_finish(1, 1, acts.at[1, 1], None, 0, 1)
    vec_y()
    reduce_end(0, 2)

    acts_out[0, s] = acts[s, 0]
    acts_out[1, s] = acts[s, 1]
    for kind in range(2):
        for i in range(2):
            cp.landed(("act", kind, i), acts_in.at[kind, :, half_of(i)])
        acts_out[kind, 1 - s] = acts_in[kind]
    for j in (1, 2, 3):
        cp.landed(("vy", j), vland.at[7 + (y + 4 - j) % 4])
    stage[4] = vland[7] + vland[8] + vland[9] + vland[10]
    vec_out[0:4] = jnp.where(s == 0, stage[4, 0:4], stage[4, 4:8])
    vec_out[4:8] = jnp.where(s == 0, stage[4, 8:12], stage[4, 12:16])
    for ch in (1, 0, 2):
        cp.landed(("rs", ch), sbuf_in.at[ch])
        w_out[ch] = sbuf[s, ch].astype(F32) + sbuf_in[ch].astype(F32)
        name = ("rs", ch)
        cp.late(name, cp.make(name, sbuf.at[1 - s, ch], sbuf_in.at[ch], to_s))
    for kind in range(2):
        for i in range(2):
            cp.late(("act", kind, i), act_copy(1 - s, kind, i))
    cp.finish()


def mega(*arguments):
    dma = pltpu.SemaphoreType.DMA
    vmem = pl.BlockSpec(memory_space=pltpu.VMEM)
    smem = pl.BlockSpec(memory_space=pltpu.SMEM)
    anywhere = pl.BlockSpec(memory_space=pl.ANY)

    def bf(*shape):
        return pltpu.VMEM(shape, BF)

    def f32(*shape):
        return pltpu.VMEM(shape, F32)

    return pl.pallas_call(
        mega_kernel,
        out_shape=[
            jax.ShapeDtypeStruct((2, 2, LOCAL, SLOT), BF),
            jax.ShapeDtypeStruct((3, 48, D), F32),
            jax.ShapeDtypeStruct((8, D), F32),
        ],
        in_specs=[smem, vmem, anywhere, anywhere] + [vmem] * 9,
        out_specs=[vmem] * 3,
        scratch_shapes=[
            bf(2, 3, D, D),
            f32(2, 8, D),
            bf(SLOT, D),
            bf(SLOT, D),
            bf(SLOT, D),
            bf(SLOT, D),
            f32(3, SLOT, 128),
            f32(SLOT, SLOT),
            f32(2, SLOT, D),
            f32(2, SLOT, 128),
            bf(2, SLOT, D),
            bf(2, SLOT, D),
            bf(2, 3, SLOT, HD),
            bf(2, 3, SLOT, HD),
            bf(2, 3, SLOT, HD),
            f32(2, 3, 128, 1280),
            bf(2, SLOT, 2 * LOCAL),
            bf(2, SLOT, D),
            f32(2, SLOT, D),
            bf(3, SLOT, HD),
            bf(SLOT, D),
            f32(SLOT, 2 * LOCAL),
            f32(SLOT, LOCAL),
            bf(SLOT, D),
            bf(SLOT, D),
            bf(2, 2, 4, 64, D),
            bf(2, 4, LOCAL, SLOT),
            bf(2, 2, 3, 64, D),
            bf(2, 3, LOCAL, SLOT),
            bf(2, 2, LOCAL, SLOT),
            bf(2, LOCAL, SLOT),
            bf(3, 8, 2, 48, D),
            bf(2, 3, 8, 48, D),
            bf(2, 4, 48, D),
            bf(2, 15, 48, D),
            bf(2, 2, 3, 48, D),
            bf(2, 3, 48, D),
            bf(3, 48, D),
            f32(16, D),
            f32(11, 16, D),
            f32(5, 16, D),
            dma((SEMS,)),
            dma((SEMS,)),
            dma((2,)),
        ],
        compiler_params=pltpu.CompilerParams(
            collective_id=0, has_side_effects=True, vmem_limit_bytes=VMEM_LIMIT
        ),
        name="two_layers",
    )(*arguments)


def hand_out_kernel(acts, sums, vec, sec, grad, wqkv, bqkv, wattn, win, bin_, wout, bout, gains, shifts):
    sec[...] = acts[0]
    grad[...] = acts[1]
    for n in range(3):
        lanes = slice(LOCAL * n, LOCAL * n + LOCAL)
        wqkv[n] = sums[2, :, lanes]
        bqkv[n] = vec[0:1, lanes]
    wattn[...] = sums[2, :, 3 * LOCAL :]
    win[...] = sums[0]
    wout[...] = sums[1]
    bin_[...] = vec[1:2, :]
    bout[...] = vec[2:3, :]
    gains[...] = vec[4:6, :]
    shifts[...] = vec[6:8, :]


def hand_out(acts, sums, vec):
    vmem = pl.BlockSpec(memory_space=pltpu.VMEM)
    shapes = [(3, 48, LOCAL), (3, 1, LOCAL), (48, LOCAL), (48, D), (1, D), (48, D), (1, D)]
    return pl.pallas_call(
        hand_out_kernel,
        out_shape=[jax.ShapeDtypeStruct((2, LOCAL, SLOT), BF)] * 2
        + [jax.ShapeDtypeStruct(shape, F32) for shape in shapes + [(2, D), (2, D)]],
        in_specs=[vmem] * 3,
        out_specs=[vmem] * 11,
        name="hand_out",
    )(acts, sums, vec)


def body(
    inputs,
    cotangent,
    seq_lengths,
    w_qkv,
    b_qkv,
    w_attn_out,
    w_in,
    b_in,
    w_out,
    b_out,
    norm_gains,
    norm_biases,
):
    powers = 1.0 / 10000.0 ** (np.arange(ROT // 2, dtype=np.float32) * 2.0 / ROT)
    freq = jnp.asarray(np.tile(powers.astype(np.float32), 128 // (ROT // 2))[None])
    acts, sums, vec = mega(
        seq_lengths[:, 0],
        freq,
        inputs,
        cotangent,
        w_qkv[0].transpose(1, 0, 2),
        w_attn_out[0].T,
        w_in[0],
        w_out[0].T,
        b_qkv.transpose(1, 0, 2),
        b_in,
        b_out,
        norm_gains[0],
        norm_biases[0],
    )
    sec, grad, wqkv, bqkv, wattn, win, bin_, wout, bout, gains, shifts = hand_out(acts, sums, vec)
    return (
        sec.transpose(0, 2, 1)[None],
        grad.transpose(0, 2, 1)[None],
        wqkv.transpose(1, 0, 2)[None],
        bqkv.transpose(1, 0, 2),
        wattn.T[None],
        win[None],
        bin_,
        wout.T[None],
        bout,
        gains[None],
        shifts[None],
    )


def solution(mesh):
    return jax.shard_map(
        body,
        mesh=mesh,
        in_specs=(
            P(None, "dp", None),
            P(None, "dp", None),
            P(None, "dp", None),
            P("section", "dp", None, "tensor"),
            P("section", None, "tensor"),
            P("section", "tensor", "dp"),
            P("section", "dp", "tensor"),
            P("section", "tensor"),
            P("section", "tensor", "dp"),
            P("section", None),
            P("section", None, None),
            P("section", None, None),
        ),
        out_specs=(
            P("section", None, "dp", "tensor"),
            P("section", None, "dp", "tensor"),
            P("section", "dp", None, "tensor"),
            P("section", None, "tensor"),
            P("section", "tensor", "dp"),
            P("section", "dp", "tensor"),
            P("section", "tensor"),
            P("section", "tensor", "dp"),
            P("section", None),
            P("section", None, None),
            P("section", None, None),
        ),
        check_vma=False,
    )
```

```python
import math

import jax
import jax.numpy as jnp
import numpy as np
from jax import lax
from jax.experimental import pallas as pl
from jax.experimental.pallas import tpu as pltpu
from jax.sharding import PartitionSpec as P

HD = 64
ROT = 16
BLOCK = 128
SEQS = 4
SLOT = 512
D = 768
LOCAL = 192
EPSILON = 1e-05
MASKED = -1e30
MESH = pl.DeviceIdType.MESH
BF = jnp.bfloat16
F32 = jnp.float32
VMEM_LIMIT = 58 * 2**20


def coords():
    dp = lax.axis_index("dp")
    return (
        lax.axis_index("section"),
        dp // 4,
        (dp // 2) % 2,
        dp % 2,
        lax.axis_index("tensor"),
    )


def dp_of(y, x, c):
    return y * 4 + x * 2 + c


def signal_all(targets):
    barrier = pltpu.get_barrier_semaphore()
    for target in targets:
        pl.semaphore_signal(barrier, inc=1, device_id=target, device_id_type=MESH)
    pl.semaphore_wait(barrier, len(targets))


def remote(src, dst, send, recv, target):
    return pltpu.make_async_remote_copy(
        src_ref=src,
        dst_ref=dst,
        send_sem=send,
        recv_sem=recv,
        device_id=target,
        device_id_type=MESH,
    )


def dot(a, b):
    return lax.dot_general(a, b, (((1,), (0,)), ((), ())), preferred_element_type=F32)


def dot_nt(a, b):
    return lax.dot_general(a, b, (((1,), (1,)), ((), ())), preferred_element_type=F32)


def dot_tn(a, b):
    return lax.dot_general(a, b, (((0,), (0,)), ((), ())), preferred_element_type=F32)


def gelu_parts(h):
    tail = 1.0 / (1.0 + (0.3275911 / math.sqrt(2.0)) * jnp.abs(h))
    bell = jnp.exp(h * h * -0.5)
    series = 0.5 * 1.061405429
    for term in (-1.453152027, 1.421413741, -0.284496736, 0.254829592):
        series = series * tail + 0.5 * term
    below = series * tail * bell
    phi = jnp.where(h >= 0.0, 1.0 - below, below)
    return h * phi, phi + h * bell * (1.0 / math.sqrt(2.0 * math.pi))


def col_sum(values):
    return jnp.sum(values, axis=0, keepdims=True)


class Copies:
    def __init__(self, send, recv, to_any):
        self.send, self.recv, self.to_any = send, recv, to_any
        self.numbers = {}
        self.sent = []
        self.done = set()

    def make(self, name, src, dst, to):
        number = self.numbers.setdefault(name, len(self.numbers))
        assert number < SEMS
        return remote(src, dst, self.send.at[number], self.recv.at[number], to)

    def start(self, name, src, dst, to):
        copy = self.make(name, src, dst, to)
        copy.start()
        self.late(name, copy)

    def late(self, name, copy):
        self.sent.append((self.numbers[name], copy))

    def landed(self, name, ref):
        self.make(name, ref, ref, self.to_any).wait_recv()

    def sent_off(self, name, src, dst, to):
        copy = self.make(name, src, dst, to)
        copy.wait_send()
        self.done.add(self.numbers[name])

    def finish(self):
        for number, copy in self.sent:
            if number not in self.done:
                copy.wait_send()


SEMS = 288
GATHER = ((2, slice(0, 384), True), (2, slice(384, D), True), (0, slice(0, D), True), (1, slice(0, D), False))
REDUCE = ((1, slice(0, D), True), (0, slice(0, D), False), (2, slice(0, 384), False), (2, slice(384, D), True))


def mega_kernel(
    len_ref,
    freq_ref,
    inputs_ref,
    cot_ref,
    wqkv_ref,
    wattn_ref,
    win_ref,
    wout_ref,
    bqkv_ref,
    bin_ref,
    bout_ref,
    gains_ref,
    shifts_ref,
    acts_out,
    w_out,
    vec_out,
    w,
    vecs,
    x0,
    x1,
    g1,
    g0,
    tables,
    bias,
    normal,
    rstd,
    na,
    nb,
    q,
    k,
    v,
    probs,
    mixp,
    act,
    slope,
    gm,
    gh,
    dqk,
    dv,
    gpre,
    full,
    zrow,
    zcol,
    zland,
    zland_c,
    acts,
    acts_in,
    grads,
    sib,
    xbuf,
    ybuf,
    keep,
    sbuf,
    sbuf_in,
    vec,
    vland,
    stage,
    send,
    recv,
    local,
):
    s, y, x, c, t = coords()
    me = dp_of(y, x, c)
    to_y = {j: {"dp": dp_of((y + j) % 4, x, c)} for j in (1, 2, 3)}
    to_z = {j: {"tensor": (t + j) % 4} for j in (1, 2, 3)}
    to_x = {"dp": dp_of(y, 1 - x, c)}
    to_c = {"dp": dp_of(y, x, 1 - c)}
    to_s = {"section": 1 - s}
    cp = Copies(send, recv, to_c)

    fetch_x = pltpu.make_async_copy(inputs_ref.at[s], x0, local.at[0])
    fetch_g = pltpu.make_async_copy(cot_ref.at[s], g1, local.at[1])
    fetch_x.start()
    fetch_g.start()

    def rows48(block):
        return pl.ds(pl.multiple_of(block * 48, 16), 48)

    w[s, 0, rows48(me), :] = win_ref[...]
    w[s, 1, rows48(me), :] = wout_ref[...]
    w[s, 2, rows48(me), :] = jnp.concatenate(
        [wqkv_ref[0], wqkv_ref[1], wqkv_ref[2], wattn_ref[...]], axis=1
    )
    vecs[s, 0:1, :] = jnp.concatenate(
        [bqkv_ref[0], bqkv_ref[1], bqkv_ref[2], jnp.zeros((1, LOCAL), F32)], axis=1
    )
    vecs[s, 1:2, :] = bin_ref[...]
    vecs[s, 2:3, :] = bout_ref[...]
    vecs[s, 3:5, :] = gains_ref[...]
    vecs[s, 5:7, :] = shifts_ref[...]
    vecs[s, 7:8, :] = jnp.zeros((1, D), F32)

    signal_all(list(to_y.values()) + list(to_z.values()) + [to_x, to_c, to_s])

    def swap(l):
        names = [("swap", ch) for ch in (2, 0, 1)]
        refs = [w.at[l, ch, rows48(me)] for ch in (2, 0, 1)]
        return [
            (name, cp.make(name, ref, ref, to_s))
            for name, ref in zip(["swap"] + names, [vecs.at[l]] + refs)
        ]

    def swap_start(l):
        @pl.when(s == l)
        def _():
            for _, copy in swap(l):
                copy.start()

    def swap_wait(l, which):
        @pl.when(s == 1 - l)
        def _():
            if which is None:
                cp.landed("swap", vecs.at[l])
            else:
                cp.landed(("swap", which), w.at[l, which, rows48(me)])

    def block_of(j, other, core=c):
        return dp_of((y + 4 - j) % 4, (1 - x) if other else x, core)

    turnwise = 1 + 2 * c
    to_relay = {"dp": dp_of((y + turnwise) % 4, x, c)}

    def part_ref(l, p, block):
        ch, lanes, _ = GATHER[p]
        return w.at[l, ch, rows48(block), lanes]

    def push(l, p, slot, block, to):
        ref = part_ref(l, p, block)
        cp.start(("w", l, p, slot), ref, ref, to)

    def arrived(l, p, slot, block):
        cp.landed(("w", l, p, slot), part_ref(l, p, block))

    def gather_first(l, p):
        if GATHER[p][2]:
            push(l, p, 0, me, to_x)
            for j in (1, 3):
                push(l, p, j, me, to_y[j])
        else:
            for j in (1, 3):
                push(l, p, j - 1, me, to_y[j])
            push(l, p, 3, me, to_x)
        push(l, p, 7, me, to_c)

    def gather_second(l, p):
        if GATHER[p][2]:
            arrived(l, p, 0, block_of(0, True))
            for j in (1, 3):
                push(l, p, 3 + j, block_of(0, True), to_y[j])
            push(l, p, 8, block_of(0, True), to_c)
        else:
            for j in (1, 3):
                arrived(l, p, j - 1, block_of(j, False))
            push(l, p, 1, block_of(turnwise, False), to_relay)
            for j in (1, 3):
                push(l, p, 3 + j, block_of(j, False), to_x)
                push(l, p, 7 + 2 * j, block_of(j, False), to_c)

    def gather_third(l, p):
        if GATHER[p][2]:
            for slot, other in ((0, False), (3, True)):
                for j in (1, 3):
                    arrived(l, p, slot + j, block_of(j, other))
                push(l, p, slot + 2, block_of(turnwise, other), to_relay)
                for j in (1, 3):
                    push(l, p, 7 + 2 * j + other, block_of(j, other), to_c)
        else:
            arrived(l, p, 1, block_of(2, False))
            push(l, p, 5, block_of(2, False), to_x)
            push(l, p, 11, block_of(2, False), to_c)
            for j in (0, 1, 3):
                arrived(l, p, 3 + j, block_of(j, True))
                push(l, p, 8 + 2 * j, block_of(j, True), to_c)

    def gather_fourth(l, p):
        if GATHER[p][2]:
            arrived(l, p, 2, block_of(2, False))
            push(l, p, 11, block_of(2, False), to_c)
        arrived(l, p, 5, block_of(2, True))
        push(l, p, 12, block_of(2, True), to_c)

    def gather_last(l, p):
        for j in range(4):
            arrived(l, p, 7 + 2 * j, block_of(j, False, 1 - c))
            arrived(l, p, 8 + 2 * j, block_of(j, True, 1 - c))

    def prepare():
        lens = [len_ref[s, j] for j in range(SEQS)]
        ends, total = [], 0
        for j in range(SEQS):
            total = total + ((lens[j] + (BLOCK - 1)) >> 7)
            ends.append(total)

        def rows_of(i, _):
            at = pl.ds(pl.multiple_of(i * 128, 128), 128)
            row = i * 128 + lax.broadcasted_iota(jnp.int32, (128, SLOT), 0)
            col = lax.broadcasted_iota(jnp.int32, (128, SLOT), 1)
            block = i
            begin = jnp.int32(0)
            owner = jnp.int32(0)
            for j in range(SEQS):
                past = (ends[j] <= block).astype(jnp.int32)
                begin = jnp.maximum(begin, past * ends[j])
                owner = owner + past
            begin = begin * BLOCK
            size = jnp.int32(0)
            for j in range(SEQS):
                size = size + (owner == j).astype(jnp.int32) * lens[j]
            fine = (col >= begin) & (col <= row) & (col < begin + size) | (col == row)
            bias[at, :] = jnp.where(fine, 0.0, MASKED)
            offset = (row[:, :128] - begin).astype(F32)
            angles = offset * freq_ref[...]
            lane = lax.broadcasted_iota(jnp.int32, (128, 128), 1) & 63
            cosines, sines = jnp.cos(angles), jnp.sin(angles)
            tables[0, at, :] = jnp.where(lane < ROT, cosines, 1.0)
            tables[1, at, :] = jnp.where(lane < ROT // 2, -sines, 0.0)
            tables[2, at, :] = jnp.where((lane >= ROT // 2) & (lane < ROT), sines, 0.0)
            return 0

        lax.fori_loop(0, 4, rows_of, 0)

    def turn(values, at, sign):
        ahead = pltpu.roll(values, 384 - ROT // 2, 1)
        behind = pltpu.roll(values, ROT // 2, 1)
        parts = []
        for b in range(3):
            lanes = slice(128 * b, 128 * b + 128)
            change = ahead[:, lanes] * tables[1, at, :] + behind[:, lanes] * tables[2, at, :]
            base = values[:, lanes] * tables[0, at, :]
            parts.append(base + change if sign > 0 else base - change)
        return jnp.concatenate(parts, axis=1)

    def norms(l, x_ref, j):
        def rows_of(i, _):
            at = pl.ds(pl.multiple_of(128 * j + i * 64, 64), 64)
            values = x_ref[at, :].astype(F32)
            centred = values - jnp.mean(values, axis=-1, keepdims=True)
            scale = lax.rsqrt(jnp.mean(centred * centred, axis=-1, keepdims=True) + EPSILON)
            unit = centred * scale
            normal[l, at, :] = unit
            rstd[l, at, :] = jnp.broadcast_to(scale, (64, 128))
            na[l, at, :] = (unit * vecs[l, 3:4, :] + vecs[l, 5:6, :]).astype(BF)
            nb[l, at, :] = (unit * vecs[l, 4:5, :] + vecs[l, 6:7, :]).astype(BF)
            return 0

        lax.fori_loop(0, 2, rows_of, 0)

    stored = [slice(64 * j * (j + 1), 64 * (j + 1) * (j + 2)) for j in range(4)]

    def project(l, first, size):
        at = slice(first, first + size)
        pre = dot(na[l, at, :], w[l, 2, :, 0 : 3 * LOCAL]) + vecs[l, 0:1, 0 : 3 * LOCAL]
        turned = turn(pre[:, 0 : 2 * LOCAL], at, 1)
        for h in range(3):
            q[l, h, at, :] = (turned[:, HD * h : HD * h + HD] * (1.0 / 8.0)).astype(BF)
            k[l, h, at, :] = turned[:, LOCAL + HD * h : LOCAL + HD * h + HD].astype(BF)
            v[l, h, at, :] = pre[:, 2 * LOCAL + HD * h : 2 * LOCAL + HD * h + HD].astype(BF)
        mixp[l, at, 0:LOCAL] = jnp.zeros((size, LOCAL), BF)

    def attend(l, j):
        rows = slice(128 * j, 128 * j + 128)
        seen = slice(0, 128 * j + 128)
        scores = [
            dot_nt(q[l, h, rows, :], k[l, h, seen, :]) + bias[rows, seen] for h in range(3)
        ]
        weights = [jnp.exp(one - jnp.max(one, axis=-1, keepdims=True)) for one in scores]
        shares = [one * (1.0 / jnp.sum(one, axis=-1, keepdims=True)) for one in weights]
        for h in range(3):
            probs[l, h, :, stored[j]] = shares[h]
        outs = [dot(shares[h].astype(BF), v[l, h, seen, :]) for h in range(3)]
        mixp[l, rows, LOCAL:] = jnp.concatenate(outs, axis=1).astype(BF)

    def feed(l, i):
        at = slice(256 * i, 256 * i + 256)
        for n in range(3):
            lanes = slice(256 * n, 256 * n + 256)
            hidden = dot(nb[l, at, :], w[l, 0, :, lanes]) + vecs[l, 1:2, lanes]
            value, grade = gelu_parts(hidden)
            act[l, at, lanes] = value.astype(BF)
            slope[l, at, lanes] = grade

    def result_rows(l, i, emit):
        rows = slice(256 * i, 256 * i + 256)
        for n in range(3):
            lanes = slice(256 * n, 256 * n + 256)
            part = dot_nt(act[l, rows, :], w[l, 1, lanes, :])
            part = part + dot_nt(mixp[l, rows, :], w[l, 2, lanes, 2 * LOCAL :])
            emit(i, lanes, part)

    def emit_row(use):
        def emit(i, lanes, part):
            for b in range(8):
                zrow[use, 2 * i + b // 4, b % 4, :, lanes] = part[32 * b : 32 * b + 32].astype(BF)

        return emit

    def emit_full(i, lanes, part):
        full[256 * i : 256 * i + 256, lanes] = part.astype(BF)

    def shared(i, b):
        return pl.ds(pl.multiple_of(128 * i + b * 32, 32), 32)

    def row_push(use, i):
        for j in (1, 3, 2):
            cp.start(
                ("zr", use, i, j), zrow.at[use, i, (t + j) % 4], zland.at[use, i, j - 1], to_z[j]
            )

    def row_finish(use, i, extra, with_bias, out_ref):
        for j in (1, 3, 2):
            cp.landed(("zr", use, i, j), zland.at[use, i, j - 1])
        here = shared(i, t)
        total = extra[here, :].astype(F32) + zrow[use, i, t].astype(F32)
        if with_bias is not None:
            total = total + vecs[with_bias, 2:3, :]
        for j in range(3):
            total = total + zland[use, i, j].astype(F32)
        out_ref[here, :] = total.astype(BF)
        for j in (1, 3, 2):
            cp.start(("za", use, i, j), out_ref.at[here], out_ref.at[here], to_z[j])

    def row_wait(use, i, out_ref):
        for j in (1, 3, 2):
            cp.landed(("za", use, i, j), out_ref.at[shared(i, (t + 4 - j) % 4)])

    def chosen(b):
        row = lax.broadcasted_iota(jnp.int32, (LOCAL, D), 0)
        return lax.broadcasted_iota(jnp.int32, (LOCAL, D), 1) == row + b * LOCAL

    def pack(ref, out):
        out[...] = dot_nt(chosen(t).astype(BF), ref[...]).astype(BF)

    def result_cols(l, use):
        for b in range(4):
            rows = slice(LOCAL * b, LOCAL * b + LOCAL)
            part = dot_nt(w[l, 1, rows, :], act[l])
            part = part + dot_nt(w[l, 2, rows, 2 * LOCAL :], mixp[l])
            zcol[use, b] = part.astype(BF)

    def part_of(i):
        return slice(128 * i, 128 * i + 128)

    def turn_cols(use, i):
        rows = slice(256 * i, 256 * i + 256)
        for b in range(4):
            zcol[use, b, :, rows] = dot_nt(chosen(b).astype(BF), full[rows, :]).astype(BF)

    def col_push(use, i):
        for j in (1, 3, 2):
            cp.start(
                ("zc", use, i, j),
                zcol.at[use, (t + j) % 4, :, part_of(i)],
                zland_c.at[use, j - 1, :, part_of(i)],
                to_z[j],
            )

    def col_finish(use, i, extra, with_bias, l, kind):
        lanes = part_of(i)
        for j in (1, 3, 2):
            cp.landed(("zc", use, i, j), zland_c.at[use, j - 1, :, lanes])
        total = extra[:, lanes].astype(F32) + zcol[use, t, :, lanes].astype(F32)
        if with_bias is not None:
            total = total + jnp.sum(
                jnp.where(chosen(t), vecs[with_bias, 2:3, :], 0.0), axis=1, keepdims=True
            )
        for j in range(3):
            total = total + zland_c[use, j, :, lanes].astype(F32)
        acts[l, kind, :, lanes] = total.astype(BF)
        act_push(l, kind, i)

    def act_copy(l, kind, i):
        ref = acts.at[l, kind, :, part_of(i)]
        return cp.make(("act", kind, i), ref, acts_in.at[kind, :, part_of(i)], to_s)

    def act_push(l, kind, i):
        @pl.when(s == 1 - l)
        def _():
            act_copy(l, kind, i).start()

    def back_heads(l, g_ref, i):
        at = slice(256 * i, 256 * i + 256)
        mixed = dot(g_ref[at, :], w[l, 2, :, 2 * LOCAL :])
        for h in range(3):
            gm[h, at, :] = mixed[:, LOCAL + HD * h : LOCAL + HD * h + HD].astype(BF)
        for n in range(3):
            lanes = slice(256 * n, 256 * n + 256)
            grad = dot(g_ref[at, :], w[l, 1, :, lanes]) * slope[l, at, lanes]
            gh[at, lanes] = grad.astype(BF)

    def back_attend(l, j):
        rows = slice(128 * j, 128 * j + 128)
        seen = slice(0, 128 * j + 128)
        shares = [probs[l, h, :, stored[j]] for h in range(3)]
        grads_of = [dot_nt(gm[h, rows, :], v[l, h, seen, :]) for h in range(3)]
        dots = [jnp.sum(shares[h] * grads_of[h], axis=-1, keepdims=True) for h in range(3)]
        grads_of = [(shares[h] * (grads_of[h] - dots[h])).astype(BF) for h in range(3)]
        by_query = [dot(grads_of[h], k[l, h, seen, :]) for h in range(3)]
        dqk[rows, 0:LOCAL] = jnp.concatenate(by_query, axis=1) * (1.0 / 8.0)
        by_key = [dot_tn(grads_of[h], q[l, h, rows, :]) for h in range(3)]
        by_value = [dot_tn(shares[h].astype(BF), gm[h, rows, :]) for h in range(3)]
        by_key = jnp.concatenate(by_key, axis=1)
        by_value = jnp.concatenate(by_value, axis=1)
        if j == 3:
            dqk[seen, LOCAL:] = by_key
            dv[seen, :] = by_value
        else:
            dqk[seen, LOCAL:] += by_key
            dv[seen, :] += by_value

    def back_turn(j):
        at = slice(128 * j, 128 * j + 128)
        gpre[at, 0 : 2 * LOCAL] = turn(dqk[at, :], at, -1).astype(BF)
        gpre[at, 2 * LOCAL :] = jnp.concatenate(
            [dv[at, :], jnp.zeros((128, LOCAL), F32)], axis=1
        ).astype(BF)

    def back_norms(l, i, emit):
        rows = slice(256 * i, 256 * i + 256)
        one = dot_nt(gpre[rows, :], w[l, 2])
        two = dot_nt(gh[rows, :], w[l, 0])
        unit = normal[l, rows, :]
        sums = [col_sum(one * unit), col_sum(two * unit), col_sum(one), col_sum(two)]
        for n, value in enumerate(sums):
            row = slice(8 + 4 * l + n, 9 + 4 * l + n)
            vec[row, :] = value if i == 1 else vec[row, :] + value
        mixture = one * vecs[l, 3:4, :] + two * vecs[l, 4:5, :]
        first = jnp.mean(mixture, axis=-1, keepdims=True)
        second = jnp.mean(mixture * unit, axis=-1, keepdims=True)
        part = rstd[l, rows, 0:1] * (mixture - first - unit * second)
        emit(i, slice(0, D), part)

    def sums_of(l, g_ref):
        for n, ref in enumerate((gpre, gh, g_ref)):
            row = slice(4 * l + n, 4 * l + n + 1)
            vec[row, :] = col_sum(ref[...].astype(F32))
        vec[4 * l + 3 : 4 * l + 4, :] = jnp.zeros((1, D), F32)

    def weights_of(l, ch, g_ref):
        def rows_of(m, _):
            lanes = pl.ds(pl.multiple_of(m * 384, 128), 384)
            if ch == 0:
                value = dot_tn(nb[l, :, lanes], gh[...])
            elif ch == 1:
                value = dot_tn(g_ref[:, lanes], act[l])
            else:
                value = dot_tn(na[l, :, lanes], gpre[...])
                other = dot_tn(g_ref[:, lanes], mixp[l])
                value = jnp.concatenate(
                    [value[:, 0 : 2 * LOCAL], value[:, 2 * LOCAL :] + other], axis=1
                )
            grads[ch, pl.ds(4 * m, 4)] = value.astype(BF).reshape(4, 2, 48, D)
            return 0

        lax.fori_loop(0, 2, rows_of, 0)
        cp.start(("rc", l, ch), grads.at[ch, :, 1 - c], sib.at[l, ch], to_c)

    def weights_gone(l, ch):
        cp.sent_off(("rc", l, ch), grads.at[ch, :, 1 - c], sib.at[l, ch], to_c)

    def reduce_core(l, ch):
        cp.landed(("rc", l, ch), sib.at[l, ch])

        def add(i, _):
            sib[l, ch, i] = (sib[l, ch, i].astype(F32) + grads[ch, i, c].astype(F32)).astype(BF)
            return 0

        lax.fori_loop(0, 8, add, 0)
        for p in range(4):
            if REDUCE[p][0] == ch:
                reduce_start(l, p)

    def reduce_start(l, p):
        ch, lanes, x_first = REDUCE[p]
        if x_first:
            for j in (1, 3, 2, 0):
                yy = (y + j) % 4
                cp.start(
                    ("rx", l, p, j),
                    sib.at[l, ch, yy * 2 + 1 - x, :, lanes],
                    xbuf.at[l, ch - 1, yy, :, lanes],
                    to_x,
                )
        else:
            for j in (1, 3, 2):
                yy = (y + j) % 4
                cp.start(
                    ("ry", l, p, j),
                    sib.at[l, ch, pl.ds(yy * 2, 2), :, lanes],
                    ybuf.at[l, pl.ds(3 * ch + 2 * (j - 1), 2), :, lanes],
                    to_y[j],
                )

    def slot_of(p, j):
        return 11 + j if REDUCE[p][0] == 1 else 5 + j

    def reduce_mid(l, p):
        ch, lanes, x_first = REDUCE[p]
        if x_first:
            for j in (1, 3, 2, 0):
                yy = (y + j) % 4
                ref = xbuf.at[l, ch - 1, yy, :, lanes]
                cp.landed(("rx", l, p, j), ref)
                mine = sib[l, ch, yy * 2 + x, :, lanes].astype(F32)
                xbuf[l, ch - 1, yy, :, lanes] = (
                    mine + xbuf[l, ch - 1, yy, :, lanes].astype(F32)
                ).astype(BF)
                if j:
                    to = ybuf.at[l, slot_of(p, j), :, lanes]
                    cp.start(("ry", l, p, j), ref, to, to_y[j])
        else:
            for j in (1, 3, 2):
                cp.landed(
                    ("ry", l, p, j), ybuf.at[l, pl.ds(3 * ch + 2 * (j - 1), 2), :, lanes]
                )
            for i in range(2):
                total = sib[l, ch, y * 2 + i, :, lanes].astype(F32)
                for j in range(3):
                    total = total + ybuf[l, 3 * ch + 2 * j + i, :, lanes].astype(F32)
                keep[l, ch // 2, i, :, lanes] = total.astype(BF)
            cp.start(
                ("rx", l, p, 0),
                keep.at[l, ch // 2, 1 - x, :, lanes],
                keep.at[l, ch // 2, 2, :, lanes],
                to_x,
            )

    def sums_copy(l, p):
        ch, lanes, _ = REDUCE[p]
        return cp.make(("rs", p), sbuf.at[l, ch, :, lanes], sbuf_in.at[ch, :, lanes], to_s)

    def reduce_end(l, p):
        ch, lanes, x_first = REDUCE[p]
        if x_first:
            total = xbuf[l, ch - 1, y, :, lanes].astype(F32)
            for j in (1, 3, 2):
                cp.landed(("ry", l, p, j), ybuf.at[l, slot_of(p, j), :, lanes])
            for j in (1, 2, 3):
                total = total + ybuf[l, slot_of(p, j), :, lanes].astype(F32)
        else:
            cp.landed(("rx", l, p, 0), keep.at[l, ch // 2, 2, :, lanes])
            total = keep[l, ch // 2, x, :, lanes].astype(F32)
            total = total + keep[l, ch // 2, 2, :, lanes].astype(F32)
        sbuf[l, ch, :, lanes] = total.astype(BF)

        @pl.when(s == 1 - l)
        def _():
            sums_copy(l, p).start()

    def vec_z():
        vland[t, 0:8] = vec[8:16, :]
        for j in (1, 2, 3):
            cp.start(("vz", j), vec.at[pl.ds(8, 8)], vland.at[t, pl.ds(0, 8)], to_z[j])

    def vec_c():
        for j in (1, 2, 3):
            cp.landed(("vz", j), vland.at[(t + 4 - j) % 4, pl.ds(0, 8)])
        stage[0, 0:8] = vec[0:8, :]
        stage[0, 8:16] = vland[0, 0:8] + vland[1, 0:8] + vland[2, 0:8] + vland[3, 0:8]
        cp.start("vc", stage.at[0], vland.at[4], to_c)

    def vec_x():
        cp.landed("vc", vland.at[4])
        stage[1] = stage[0] + vland[4]
        cp.start("vx", stage.at[1], vland.at[5], to_x)

    def vec_s():
        cp.landed("vx", vland.at[5])
        stage[2] = stage[1] + vland[5]
        cp.start("vs", stage.at[2], vland.at[6], to_s)

    def vec_y():
        cp.landed("vs", vland.at[6])
        stage[3] = stage[2] + vland[6]
        vland[7 + y] = stage[3]
        for j in (1, 2, 3):
            cp.start(("vy", j), stage.at[3], vland.at[7 + y], to_y[j])

    swap_start(0)
    swap_wait(0, 2)
    gather_first(0, 0)
    gather_first(0, 1)
    prepare()
    gather_second(0, 0)
    gather_second(0, 1)
    swap_wait(0, 0)
    gather_first(0, 2)
    swap_wait(0, 1)
    gather_first(0, 3)
    swap_wait(0, None)
    swap_start(1)
    fetch_x.wait()
    norms(0, x0, 0)
    norms(0, x0, 1)
    gather_third(0, 0)
    gather_third(0, 1)
    norms(0, x0, 2)
    norms(0, x0, 3)
    gather_second(0, 2)
    gather_second(0, 3)
    gather_fourth(0, 0)
    gather_fourth(0, 1)
    gather_last(0, 0)
    gather_last(0, 1)
    project(0, 0, 256)
    project(0, 256, 256)
    attend(0, 0)
    gather_third(0, 2)
    gather_third(0, 3)
    swap_wait(1, 2)
    gather_first(1, 0)
    gather_first(1, 1)
    swap_wait(1, 0)
    gather_first(1, 2)
    swap_wait(1, 1)
    gather_first(1, 3)
    swap_wait(1, None)
    attend(0, 1)
    gather_fourth(0, 2)
    gather_fourth(0, 3)
    attend(0, 2)
    gather_second(1, 0)
    gather_second(1, 1)
    attend(0, 3)
    gather_second(1, 2)
    gather_second(1, 3)
    gather_last(0, 2)
    feed(0, 0)
    gather_last(0, 3)
    result_rows(0, 0, emit_row(0))
    row_push(0, 0)
    row_push(0, 1)
    gather_third(1, 0)
    gather_third(1, 1)
    feed(0, 1)
    result_rows(0, 1, emit_row(0))
    row_push(0, 2)
    row_push(0, 3)
    row_finish(0, 0, x0, 0, x1)
    row_finish(0, 1, x0, 0, x1)
    gather_third(1, 2)
    row_finish(0, 2, x0, 0, x1)
    gather_third(1, 3)
    row_finish(0, 3, x0, 0, x1)
    for p in range(4):
        gather_fourth(1, p)
    gather_last(1, 0)
    gather_last(1, 1)

    for i in range(2):
        row_wait(0, 2 * i, x1)
        norms(1, x1, 2 * i)
        row_wait(0, 2 * i + 1, x1)
        norms(1, x1, 2 * i + 1)
        project(1, 256 * i, 256)
        attend(1, 2 * i)
        attend(1, 2 * i + 1)
        if i == 0:
            gather_last(1, 2)
        feed(1, i)
    gather_last(1, 3)

    fetch_g.wait()
    back_heads(1, g1, 1)
    back_heads(1, g1, 0)
    for i in (1, 0):
        back_attend(1, 2 * i + 1)
        back_attend(1, 2 * i)
        back_turn(2 * i + 1)
        back_turn(2 * i)
        back_norms(1, i, emit_row(1))
        row_push(1, 2 * i + 1)
        row_push(1, 2 * i)
    row_finish(1, 3, g1, None, g0)
    weights_of(1, 1, g1)
    row_finish(1, 2, g1, None, g0)
    weights_of(1, 0, g1)
    row_finish(1, 1, g1, None, g0)
    weights_of(1, 2, g1)
    row_finish(1, 0, g1, None, g0)
    reduce_core(1, 1)
    reduce_core(1, 0)
    sums_of(1, g1)
    reduce_core(1, 2)
    result_cols(1, 0)
    for i in range(4):
        col_push(0, i)
    pack(x1, acts.at[0, 0])
    for i in range(4):
        act_push(0, 0, i)
    for ch in range(3):
        weights_gone(1, ch)

    for i in (1, 0):
        row_wait(1, 2 * i + 1, g0)
        row_wait(1, 2 * i, g0)
        back_heads(0, g0, i)
        if i == 0:
            weights_of(0, 1, g0)
            weights_of(0, 0, g0)
            reduce_mid(1, 1)
            reduce_mid(1, 2)
            reduce_mid(1, 3)
            reduce_core(0, 1)
            pack(g0, acts.at[1, 1])
            for n in range(4):
                act_push(1, 1, n)
        back_attend(0, 2 * i + 1)
        if i == 1:
            reduce_mid(1, 0)
        else:
            reduce_core(0, 0)
        back_attend(0, 2 * i)
        if i == 1:
            for n in range(4):
                col_finish(0, n, acts.at[0, 0], 1, 1, 0)
        back_turn(2 * i + 1)
        back_turn(2 * i)
        back_norms(0, i, emit_full)
        turn_cols(1, i)
        col_push(1, 2 * i + 1)
        col_push(1, 2 * i)
    weights_of(0, 2, g0)
    for p in range(4):
        reduce_end(1, p)
    sums_of(0, g0)
    vec_z()
    reduce_core(0, 2)
    vec_c()
    reduce_mid(0, 0)
    reduce_mid(0, 1)
    vec_x()
    col_finish(1, 3, acts.at[1, 1], None, 0, 1)
    col_finish(1, 2, acts.at[1, 1], None, 0, 1)
    vec_s()
    reduce_mid(0, 3)
    reduce_end(0, 1)
    reduce_mid(0, 2)
    reduce_end(0, 0)
    col_finish(1, 1, acts.at[1, 1], None, 0, 1)
    col_finish(1, 0, acts.at[1, 1], None, 0, 1)
    vec_y()
    reduce_end(0, 3)
    reduce_end(0, 2)

    acts_out[0, s] = acts[s, 0]
    acts_out[1, s] = acts[s, 1]
    for kind in range(2):
        for i in range(4):
            cp.landed(("act", kind, i), acts_in.at[kind, :, part_of(i)])
        acts_out[kind, 1 - s] = acts_in[kind]
    for j in (1, 2, 3):
        cp.landed(("vy", j), vland.at[7 + (y + 4 - j) % 4])
    stage[4] = vland[7] + vland[8] + vland[9] + vland[10]
    vec_out[0:4] = jnp.where(s == 0, stage[4, 0:4], stage[4, 4:8])
    vec_out[4:8] = jnp.where(s == 0, stage[4, 8:12], stage[4, 12:16])
    for p, (ch, lanes, _) in enumerate(REDUCE):
        cp.landed(("rs", p), sbuf_in.at[ch, :, lanes])
        w_out[ch, :, lanes] = sbuf[s, ch, :, lanes].astype(F32) + sbuf_in[ch, :, lanes].astype(F32)
        cp.late(("rs", p), sums_copy(1 - s, p))
    for name, copy in swap(s):
        cp.late(name, copy)
    for kind in range(2):
        for i in range(4):
            cp.late(("act", kind, i), act_copy(1 - s, kind, i))
    cp.finish()


def mega(*arguments):
    dma = pltpu.SemaphoreType.DMA
    vmem = pl.BlockSpec(memory_space=pltpu.VMEM)
    smem = pl.BlockSpec(memory_space=pltpu.SMEM)
    anywhere = pl.BlockSpec(memory_space=pl.ANY)

    def bf(*shape):
        return pltpu.VMEM(shape, BF)

    def f32(*shape):
        return pltpu.VMEM(shape, F32)

    return pl.pallas_call(
        mega_kernel,
        out_shape=[
            jax.ShapeDtypeStruct((2, 2, LOCAL, SLOT), BF),
            jax.ShapeDtypeStruct((3, 48, D), F32),
            jax.ShapeDtypeStruct((8, D), F32),
        ],
        in_specs=[smem, vmem, anywhere, anywhere] + [vmem] * 9,
        out_specs=[vmem] * 3,
        scratch_shapes=[
            bf(2, 3, D, D),
            f32(2, 8, D),
            bf(SLOT, D),
            bf(SLOT, D),
            bf(SLOT, D),
            bf(SLOT, D),
            f32(3, SLOT, 128),
            f32(SLOT, SLOT),
            f32(2, SLOT, D),
            f32(2, SLOT, 128),
            bf(2, SLOT, D),
            bf(2, SLOT, D),
            bf(2, 3, SLOT, HD),
            bf(2, 3, SLOT, HD),
            bf(2, 3, SLOT, HD),
            f32(2, 3, 128, 1280),
            bf(2, SLOT, 2 * LOCAL),
            bf(2, SLOT, D),
            f32(2, SLOT, D),
            bf(3, SLOT, HD),
            bf(SLOT, D),
            f32(SLOT, 2 * LOCAL),
            f32(SLOT, LOCAL),
            bf(SLOT, D),
            bf(SLOT, D),
            bf(2, 4, 4, 32, D),
            bf(2, 4, LOCAL, SLOT),
            bf(2, 4, 3, 32, D),
            bf(2, 3, LOCAL, SLOT),
            bf(2, 2, LOCAL, SLOT),
            bf(2, LOCAL, SLOT),
            bf(3, 8, 2, 48, D),
            bf(2, 3, 8, 48, D),
            bf(2, 2, 4, 48, D),
            bf(2, 15, 48, D),
            bf(2, 2, 3, 48, D),
            bf(2, 3, 48, D),
            bf(3, 48, D),
            f32(16, D),
            f32(11, 16, D),
            f32(5, 16, D),
            dma((SEMS,)),
            dma((SEMS,)),
            dma((2,)),
        ],
        compiler_params=pltpu.CompilerParams(
            collective_id=0, has_side_effects=True, vmem_limit_bytes=VMEM_LIMIT
        ),
        name="two_layers",
    )(*arguments)


def hand_out_kernel(acts, sums, vec, sec, grad, wqkv, bqkv, wattn, win, bin_, wout, bout, gains, shifts):
    sec[...] = acts[0]
    grad[...] = acts[1]
    for n in range(3):
        lanes = slice(LOCAL * n, LOCAL * n + LOCAL)
        wqkv[n] = sums[2, :, lanes]
        bqkv[n] = vec[0:1, lanes]
    wattn[...] = sums[2, :, 3 * LOCAL :]
    win[...] = sums[0]
    wout[...] = sums[1]
    bin_[...] = vec[1:2, :]
    bout[...] = vec[2:3, :]
    gains[...] = vec[4:6, :]
    shifts[...] = vec[6:8, :]


def hand_out(acts, sums, vec):
    vmem = pl.BlockSpec(memory_space=pltpu.VMEM)
    shapes = [(3, 48, LOCAL), (3, 1, LOCAL), (48, LOCAL), (48, D), (1, D), (48, D), (1, D)]
    return pl.pallas_call(
        hand_out_kernel,
        out_shape=[jax.ShapeDtypeStruct((2, LOCAL, SLOT), BF)] * 2
        + [jax.ShapeDtypeStruct(shape, F32) for shape in shapes + [(2, D), (2, D)]],
        in_specs=[vmem] * 3,
        out_specs=[vmem] * 11,
        name="hand_out",
    )(acts, sums, vec)


def body(
    inputs,
    cotangent,
    seq_lengths,
    w_qkv,
    b_qkv,
    w_attn_out,
    w_in,
    b_in,
    w_out,
    b_out,
    norm_gains,
    norm_biases,
):
    powers = 1.0 / 10000.0 ** (np.arange(ROT // 2, dtype=np.float32) * 2.0 / ROT)
    freq = jnp.asarray(np.tile(powers.astype(np.float32), 128 // (ROT // 2))[None])
    acts, sums, vec = mega(
        seq_lengths[:, 0],
        freq,
        inputs,
        cotangent,
        w_qkv[0].transpose(1, 0, 2),
        w_attn_out[0].T,
        w_in[0],
        w_out[0].T,
        b_qkv.transpose(1, 0, 2),
        b_in,
        b_out,
        norm_gains[0],
        norm_biases[0],
    )
    sec, grad, wqkv, bqkv, wattn, win, bin_, wout, bout, gains, shifts = hand_out(acts, sums, vec)
    return (
        sec.transpose(0, 2, 1)[None],
        grad.transpose(0, 2, 1)[None],
        wqkv.transpose(1, 0, 2)[None],
        bqkv.transpose(1, 0, 2),
        wattn.T[None],
        win[None],
        bin_,
        wout.T[None],
        bout,
        gains[None],
        shifts[None],
    )


def solution(mesh):
    return jax.shard_map(
        body,
        mesh=mesh,
        in_specs=(
            P(None, "dp", None),
            P(None, "dp", None),
            P(None, "dp", None),
            P("section", "dp", None, "tensor"),
            P("section", None, "tensor"),
            P("section", "tensor", "dp"),
            P("section", "dp", "tensor"),
            P("section", "tensor"),
            P("section", "tensor", "dp"),
            P("section", None),
            P("section", None, None),
            P("section", None, None),
        ),
        out_specs=(
            P("section", None, "dp", "tensor"),
            P("section", None, "dp", "tensor"),
            P("section", "dp", None, "tensor"),
            P("section", None, "tensor"),
            P("section", "tensor", "dp"),
            P("section", "dp", "tensor"),
            P("section", "tensor"),
            P("section", "tensor", "dp"),
            P("section", None),
            P("section", None, None),
            P("section", None, None),
        ),
        check_vma=False,
    )
```

```python
import math

import jax
import jax.numpy as jnp
import numpy as np
from jax import lax
from jax.experimental import pallas as pl
from jax.experimental.pallas import tpu as pltpu
from jax.sharding import PartitionSpec as P

HD = 64
ROT = 16
BLOCK = 128
SEQS = 4
SLOT = 512
D = 768
LOCAL = 192
EPSILON = 1e-05
MASKED = -1e30
MESH = pl.DeviceIdType.MESH
BF = jnp.bfloat16
F32 = jnp.float32
VMEM_LIMIT = 58 * 2**20


def coords():
    dp = lax.axis_index("dp")
    return (
        lax.axis_index("section"),
        dp // 4,
        (dp // 2) % 2,
        dp % 2,
        lax.axis_index("tensor"),
    )


def dp_of(y, x, c):
    return y * 4 + x * 2 + c


def signal_all(targets):
    barrier = pltpu.get_barrier_semaphore()
    for target in targets:
        pl.semaphore_signal(barrier, inc=1, device_id=target, device_id_type=MESH)
    pl.semaphore_wait(barrier, len(targets))


def remote(src, dst, send, recv, target):
    return pltpu.make_async_remote_copy(
        src_ref=src,
        dst_ref=dst,
        send_sem=send,
        recv_sem=recv,
        device_id=target,
        device_id_type=MESH,
    )


def dot(a, b):
    return lax.dot_general(a, b, (((1,), (0,)), ((), ())), preferred_element_type=F32)


def dot_nt(a, b):
    return lax.dot_general(a, b, (((1,), (1,)), ((), ())), preferred_element_type=F32)


def dot_tn(a, b):
    return lax.dot_general(a, b, (((0,), (0,)), ((), ())), preferred_element_type=F32)


def gelu_parts(h):
    tail = 1.0 / (1.0 + (0.3275911 / math.sqrt(2.0)) * jnp.abs(h))
    bell = jnp.exp(h * h * -0.5)
    series = 0.5 * 1.061405429
    for term in (-1.453152027, 1.421413741, -0.284496736, 0.254829592):
        series = series * tail + 0.5 * term
    below = series * tail * bell
    phi = jnp.where(h >= 0.0, 1.0 - below, below)
    return h * phi, phi + h * bell * (1.0 / math.sqrt(2.0 * math.pi))


def col_sum(values):
    return jnp.sum(values, axis=0, keepdims=True)


class Copies:
    def __init__(self, send, recv, to_any):
        self.send, self.recv, self.to_any = send, recv, to_any
        self.numbers = {}
        self.sent = []
        self.done = set()

    def make(self, name, src, dst, to):
        number = self.numbers.setdefault(name, len(self.numbers))
        assert number < SEMS
        return remote(src, dst, self.send.at[number], self.recv.at[number], to)

    def start(self, name, src, dst, to):
        copy = self.make(name, src, dst, to)
        copy.start()
        self.late(name, copy)

    def late(self, name, copy):
        self.sent.append((self.numbers[name], copy))

    def landed(self, name, ref):
        self.make(name, ref, ref, self.to_any).wait_recv()

    def sent_off(self, name, src, dst, to):
        copy = self.make(name, src, dst, to)
        copy.wait_send()
        self.done.add(self.numbers[name])

    def finish(self):
        for number, copy in self.sent:
            if number not in self.done:
                copy.wait_send()


SEMS = 288
GATHER = ((2, slice(0, 384), True), (2, slice(384, D), True), (0, slice(0, D), True), (1, slice(0, D), False))
REDUCE = ((1, slice(0, D), True), (0, slice(0, D), False), (2, slice(0, 384), False), (2, slice(384, D), True))


def mega_kernel(
    len_ref,
    freq_ref,
    inputs_ref,
    cot_ref,
    wqkv_ref,
    wattn_ref,
    win_ref,
    wout_ref,
    bqkv_ref,
    bin_ref,
    bout_ref,
    gains_ref,
    shifts_ref,
    acts_out,
    w_out,
    vec_out,
    w,
    vecs,
    x0,
    x1,
    g1,
    g0,
    tables,
    bias,
    normal,
    rstd,
    na,
    nb,
    q,
    k,
    v,
    probs,
    mixp,
    act,
    slope,
    gm,
    gh,
    dqk,
    dv,
    gpre,
    full,
    zrow,
    zcol,
    zland,
    zland_c,
    acts,
    acts_in,
    grads,
    sib,
    xbuf,
    ybuf,
    keep,
    sbuf,
    sbuf_in,
    vec,
    vland,
    stage,
    send,
    recv,
    local,
):
    s, y, x, c, t = coords()
    me = dp_of(y, x, c)
    to_y = {j: {"dp": dp_of((y + j) % 4, x, c)} for j in (1, 2, 3)}
    to_z = {j: {"tensor": (t + j) % 4} for j in (1, 2, 3)}
    to_x = {"dp": dp_of(y, 1 - x, c)}
    to_c = {"dp": dp_of(y, x, 1 - c)}
    to_s = {"section": 1 - s}
    cp = Copies(send, recv, to_c)

    fetch_x = pltpu.make_async_copy(inputs_ref.at[s], x0, local.at[0])
    fetch_g = pltpu.make_async_copy(cot_ref.at[s], g1, local.at[1])
    fetch_x.start()
    fetch_g.start()

    def rows48(block):
        return pl.ds(pl.multiple_of(block * 48, 16), 48)

    w[s, 0, rows48(me), :] = win_ref[...]
    w[s, 1, rows48(me), :] = wout_ref[...]
    w[s, 2, rows48(me), :] = jnp.concatenate(
        [wqkv_ref[0], wqkv_ref[1], wqkv_ref[2], wattn_ref[...]], axis=1
    )
    vecs[s, 0:1, :] = jnp.concatenate(
        [bqkv_ref[0], bqkv_ref[1], bqkv_ref[2], jnp.zeros((1, LOCAL), F32)], axis=1
    )
    vecs[s, 1:2, :] = bin_ref[...]
    vecs[s, 2:3, :] = bout_ref[...]
    vecs[s, 3:5, :] = gains_ref[...]
    vecs[s, 5:7, :] = shifts_ref[...]
    vecs[s, 7:8, :] = jnp.zeros((1, D), F32)

    signal_all(list(to_y.values()) + list(to_z.values()) + [to_x, to_c, to_s])

    def swap(l):
        names = [("swap", ch) for ch in (2, 0, 1)]
        refs = [w.at[l, ch, rows48(me)] for ch in (2, 0, 1)]
        return [
            (name, cp.make(name, ref, ref, to_s))
            for name, ref in zip(["swap"] + names, [vecs.at[l]] + refs)
        ]

    def swap_start(l):
        @pl.when(s == l)
        def _():
            for _, copy in swap(l):
                copy.start()

    def swap_wait(l, which):
        @pl.when(s == 1 - l)
        def _():
            if which is None:
                cp.landed("swap", vecs.at[l])
            else:
                cp.landed(("swap", which), w.at[l, which, rows48(me)])

    def block_of(j, other, core=c):
        return dp_of((y + 4 - j) % 4, (1 - x) if other else x, core)

    turnwise = 1 + 2 * c
    to_relay = {"dp": dp_of((y + turnwise) % 4, x, c)}

    def part_ref(l, p, block):
        ch, lanes, _ = GATHER[p]
        return w.at[l, ch, rows48(block), lanes]

    def push(l, p, slot, block, to):
        ref = part_ref(l, p, block)
        cp.start(("w", l, p, slot), ref, ref, to)

    def arrived(l, p, slot, block):
        cp.landed(("w", l, p, slot), part_ref(l, p, block))

    def gather_first(l, p):
        if GATHER[p][2]:
            push(l, p, 0, me, to_x)
            for j in (1, 3):
                push(l, p, j, me, to_y[j])
        else:
            for j in (1, 3):
                push(l, p, j - 1, me, to_y[j])
            push(l, p, 3, me, to_x)
        push(l, p, 7, me, to_c)

    def gather_second(l, p):
        if GATHER[p][2]:
            arrived(l, p, 0, block_of(0, True))
            for j in (1, 3):
                push(l, p, 3 + j, block_of(0, True), to_y[j])
            push(l, p, 8, block_of(0, True), to_c)
        else:
            for j in (1, 3):
                arrived(l, p, j - 1, block_of(j, False))
            push(l, p, 1, block_of(turnwise, False), to_relay)
            for j in (1, 3):
                push(l, p, 3 + j, block_of(j, False), to_x)
                push(l, p, 7 + 2 * j, block_of(j, False), to_c)

    def gather_third(l, p):
        if GATHER[p][2]:
            for slot, other in ((0, False), (3, True)):
                for j in (1, 3):
                    arrived(l, p, slot + j, block_of(j, other))
                push(l, p, slot + 2, block_of(turnwise, other), to_relay)
                for j in (1, 3):
                    push(l, p, 7 + 2 * j + other, block_of(j, other), to_c)
        else:
            arrived(l, p, 1, block_of(2, False))
            push(l, p, 5, block_of(2, False), to_x)
            push(l, p, 11, block_of(2, False), to_c)
            for j in (0, 1, 3):
                arrived(l, p, 3 + j, block_of(j, True))
                push(l, p, 8 + 2 * j, block_of(j, True), to_c)

    def gather_fourth(l, p):
        if GATHER[p][2]:
            arrived(l, p, 2, block_of(2, False))
            push(l, p, 11, block_of(2, False), to_c)
        arrived(l, p, 5, block_of(2, True))
        push(l, p, 12, block_of(2, True), to_c)

    def gather_last(l, p):
        for j in range(4):
            arrived(l, p, 7 + 2 * j, block_of(j, False, 1 - c))
            arrived(l, p, 8 + 2 * j, block_of(j, True, 1 - c))

    def prepare():
        lens = [len_ref[s, j] for j in range(SEQS)]
        ends, total = [], 0
        for j in range(SEQS):
            total = total + ((lens[j] + (BLOCK - 1)) >> 7)
            ends.append(total)

        def rows_of(i, _):
            at = pl.ds(pl.multiple_of(i * 128, 128), 128)
            row = i * 128 + lax.broadcasted_iota(jnp.int32, (128, SLOT), 0)
            col = lax.broadcasted_iota(jnp.int32, (128, SLOT), 1)
            block = i
            begin = jnp.int32(0)
            owner = jnp.int32(0)
            for j in range(SEQS):
                past = (ends[j] <= block).astype(jnp.int32)
                begin = jnp.maximum(begin, past * ends[j])
                owner = owner + past
            begin = begin * BLOCK
            size = jnp.int32(0)
            for j in range(SEQS):
                size = size + (owner == j).astype(jnp.int32) * lens[j]
            fine = (col >= begin) & (col <= row) & (col < begin + size) | (col == row)
            bias[at, :] = jnp.where(fine, 0.0, MASKED)
            offset = (row[:, :128] - begin).astype(F32)
            angles = offset * freq_ref[...]
            lane = lax.broadcasted_iota(jnp.int32, (128, 128), 1) & 63
            cosines, sines = jnp.cos(angles), jnp.sin(angles)
            tables[0, at, :] = jnp.where(lane < ROT, cosines, 1.0)
            tables[1, at, :] = jnp.where(lane < ROT // 2, -sines, 0.0)
            tables[2, at, :] = jnp.where((lane >= ROT // 2) & (lane < ROT), sines, 0.0)
            return 0

        lax.fori_loop(0, 4, rows_of, 0)

    def turn(values, at, sign):
        ahead = pltpu.roll(values, 384 - ROT // 2, 1)
        behind = pltpu.roll(values, ROT // 2, 1)
        parts = []
        for b in range(3):
            lanes = slice(128 * b, 128 * b + 128)
            change = ahead[:, lanes] * tables[1, at, :] + behind[:, lanes] * tables[2, at, :]
            base = values[:, lanes] * tables[0, at, :]
            parts.append(base + change if sign > 0 else base - change)
        return jnp.concatenate(parts, axis=1)

    def norms(l, x_ref, j):
        def rows_of(i, _):
            at = pl.ds(pl.multiple_of(128 * j + i * 64, 64), 64)
            values = x_ref[at, :].astype(F32)
            centred = values - jnp.mean(values, axis=-1, keepdims=True)
            scale = lax.rsqrt(jnp.mean(centred * centred, axis=-1, keepdims=True) + EPSILON)
            unit = centred * scale
            normal[l, at, :] = unit
            rstd[l, at, :] = jnp.broadcast_to(scale, (64, 128))
            na[l, at, :] = (unit * vecs[l, 3:4, :] + vecs[l, 5:6, :]).astype(BF)
            nb[l, at, :] = (unit * vecs[l, 4:5, :] + vecs[l, 6:7, :]).astype(BF)
            return 0

        lax.fori_loop(0, 2, rows_of, 0)

    stored = [slice(64 * j * (j + 1), 64 * (j + 1) * (j + 2)) for j in range(4)]

    def project(l, first, size):
        at = slice(first, first + size)
        pre = dot(na[l, at, :], w[l, 2, :, 0 : 3 * LOCAL]) + vecs[l, 0:1, 0 : 3 * LOCAL]
        turned = turn(pre[:, 0 : 2 * LOCAL], at, 1)
        for h in range(3):
            q[l, h, at, :] = (turned[:, HD * h : HD * h + HD] * (1.0 / 8.0)).astype(BF)
            k[l, h, at, :] = turned[:, LOCAL + HD * h : LOCAL + HD * h + HD].astype(BF)
            v[l, h, at, :] = pre[:, 2 * LOCAL + HD * h : 2 * LOCAL + HD * h + HD].astype(BF)
        mixp[l, at, 0:LOCAL] = jnp.zeros((size, LOCAL), BF)

    def attend(l, *blocks):
        work = [
            (j, h, slice(128 * j, 128 * j + 128), slice(0, 128 * j + 128))
            for j in blocks
            for h in range(3)
        ]
        scores = [
            dot_nt(q[l, h, rows, :], k[l, h, seen, :]) + bias[rows, seen]
            for _, h, rows, seen in work
        ]
        weights = [jnp.exp(one - jnp.max(one, axis=-1, keepdims=True)) for one in scores]
        shares = [one * (1.0 / jnp.sum(one, axis=-1, keepdims=True)) for one in weights]
        for (j, h, _, _), share in zip(work, shares):
            probs[l, h, :, stored[j]] = share
        outs = [
            dot(share.astype(BF), v[l, h, seen, :])
            for (_, h, _, seen), share in zip(work, shares)
        ]
        for n, j in enumerate(blocks):
            mixp[l, 128 * j : 128 * j + 128, LOCAL:] = jnp.concatenate(
                outs[3 * n : 3 * n + 3], axis=1
            ).astype(BF)

    def feed(l, i):
        at = slice(256 * i, 256 * i + 256)
        for n in range(3):
            lanes = slice(256 * n, 256 * n + 256)
            hidden = dot(nb[l, at, :], w[l, 0, :, lanes]) + vecs[l, 1:2, lanes]
            value, grade = gelu_parts(hidden)
            act[l, at, lanes] = value.astype(BF)
            slope[l, at, lanes] = grade

    def result_rows(l, i, emit):
        rows = slice(256 * i, 256 * i + 256)
        for n in range(3):
            lanes = slice(256 * n, 256 * n + 256)
            part = dot_nt(act[l, rows, :], w[l, 1, lanes, :])
            part = part + dot_nt(mixp[l, rows, :], w[l, 2, lanes, 2 * LOCAL :])
            emit(i, lanes, part)

    def emit_row(use):
        def emit(i, lanes, part):
            for b in range(8):
                zrow[use, 2 * i + b // 4, b % 4, :, lanes] = part[32 * b : 32 * b + 32].astype(BF)

        return emit

    def emit_full(i, lanes, part):
        full[256 * i : 256 * i + 256, lanes] = part.astype(BF)

    def shared(i, b):
        return pl.ds(pl.multiple_of(128 * i + b * 32, 32), 32)

    def row_push(use, i):
        for j in (1, 3, 2):
            cp.start(
                ("zr", use, i, j), zrow.at[use, i, (t + j) % 4], zland.at[use, i, j - 1], to_z[j]
            )

    def row_finish(use, i, extra, with_bias, out_ref):
        for j in (1, 3, 2):
            cp.landed(("zr", use, i, j), zland.at[use, i, j - 1])
        here = shared(i, t)
        total = extra[here, :].astype(F32) + zrow[use, i, t].astype(F32)
        if with_bias is not None:
            total = total + vecs[with_bias, 2:3, :]
        for j in range(3):
            total = total + zland[use, i, j].astype(F32)
        out_ref[here, :] = total.astype(BF)
        for j in (1, 3, 2):
            cp.start(("za", use, i, j), out_ref.at[here], out_ref.at[here], to_z[j])

    def row_wait(use, i, out_ref):
        for j in (1, 3, 2):
            cp.landed(("za", use, i, j), out_ref.at[shared(i, (t + 4 - j) % 4)])

    def chosen(b):
        row = lax.broadcasted_iota(jnp.int32, (LOCAL, D), 0)
        return lax.broadcasted_iota(jnp.int32, (LOCAL, D), 1) == row + b * LOCAL

    def pack(ref, out):
        out[...] = dot_nt(chosen(t).astype(BF), ref[...]).astype(BF)

    def result_cols(l, use):
        for b in range(4):
            rows = slice(LOCAL * b, LOCAL * b + LOCAL)
            part = dot_nt(w[l, 1, rows, :], act[l])
            part = part + dot_nt(w[l, 2, rows, 2 * LOCAL :], mixp[l])
            zcol[use, b] = part.astype(BF)

    def part_of(i):
        return slice(128 * i, 128 * i + 128)

    def turn_cols(use, i):
        rows = slice(256 * i, 256 * i + 256)
        for b in range(4):
            zcol[use, b, :, rows] = dot_nt(chosen(b).astype(BF), full[rows, :]).astype(BF)

    def col_push(use, i):
        for j in (1, 3, 2):
            cp.start(
                ("zc", use, i, j),
                zcol.at[use, (t + j) % 4, :, part_of(i)],
                zland_c.at[use, j - 1, :, part_of(i)],
                to_z[j],
            )

    def col_finish(use, i, extra, with_bias, l, kind):
        lanes = part_of(i)
        for j in (1, 3, 2):
            cp.landed(("zc", use, i, j), zland_c.at[use, j - 1, :, lanes])
        total = extra[:, lanes].astype(F32) + zcol[use, t, :, lanes].astype(F32)
        if with_bias is not None:
            total = total + jnp.sum(
                jnp.where(chosen(t), vecs[with_bias, 2:3, :], 0.0), axis=1, keepdims=True
            )
        for j in range(3):
            total = total + zland_c[use, j, :, lanes].astype(F32)
        acts[l, kind, :, lanes] = total.astype(BF)
        act_push(l, kind, i)

    def act_copy(l, kind, i):
        ref = acts.at[l, kind, :, part_of(i)]
        return cp.make(("act", kind, i), ref, acts_in.at[kind, :, part_of(i)], to_s)

    def act_push(l, kind, i):
        @pl.when(s == 1 - l)
        def _():
            act_copy(l, kind, i).start()

    def back_heads(l, g_ref, i):
        at = slice(256 * i, 256 * i + 256)
        mixed = dot(g_ref[at, :], w[l, 2, :, 2 * LOCAL :])
        for h in range(3):
            gm[h, at, :] = mixed[:, LOCAL + HD * h : LOCAL + HD * h + HD].astype(BF)
        for n in range(3):
            lanes = slice(256 * n, 256 * n + 256)
            grad = dot(g_ref[at, :], w[l, 1, :, lanes]) * slope[l, at, lanes]
            gh[at, lanes] = grad.astype(BF)

    def back_attend(l, j):
        rows = slice(128 * j, 128 * j + 128)
        seen = slice(0, 128 * j + 128)
        shares = [probs[l, h, :, stored[j]] for h in range(3)]
        grads_of = [dot_nt(gm[h, rows, :], v[l, h, seen, :]) for h in range(3)]
        dots = [jnp.sum(shares[h] * grads_of[h], axis=-1, keepdims=True) for h in range(3)]
        grads_of = [(shares[h] * (grads_of[h] - dots[h])).astype(BF) for h in range(3)]
        by_query = [dot(grads_of[h], k[l, h, seen, :]) for h in range(3)]
        dqk[rows, 0:LOCAL] = jnp.concatenate(by_query, axis=1) * (1.0 / 8.0)
        by_key = [dot_tn(grads_of[h], q[l, h, rows, :]) for h in range(3)]
        by_value = [dot_tn(shares[h].astype(BF), gm[h, rows, :]) for h in range(3)]
        by_key = jnp.concatenate(by_key, axis=1)
        by_value = jnp.concatenate(by_value, axis=1)
        if j == 3:
            dqk[seen, LOCAL:] = by_key
            dv[seen, :] = by_value
        else:
            dqk[seen, LOCAL:] += by_key
            dv[seen, :] += by_value

    def back_turn(j):
        at = slice(128 * j, 128 * j + 128)
        gpre[at, 0 : 2 * LOCAL] = turn(dqk[at, :], at, -1).astype(BF)
        gpre[at, 2 * LOCAL :] = jnp.concatenate(
            [dv[at, :], jnp.zeros((128, LOCAL), F32)], axis=1
        ).astype(BF)

    def back_norms(l, i, emit):
        rows = slice(256 * i, 256 * i + 256)
        one = dot_nt(gpre[rows, :], w[l, 2])
        two = dot_nt(gh[rows, :], w[l, 0])
        unit = normal[l, rows, :]
        sums = [col_sum(one * unit), col_sum(two * unit), col_sum(one), col_sum(two)]
        for n, value in enumerate(sums):
            row = slice(8 + 4 * l + n, 9 + 4 * l + n)
            vec[row, :] = value if i == 1 else vec[row, :] + value
        mixture = one * vecs[l, 3:4, :] + two * vecs[l, 4:5, :]
        first = jnp.mean(mixture, axis=-1, keepdims=True)
        second = jnp.mean(mixture * unit, axis=-1, keepdims=True)
        part = rstd[l, rows, 0:1] * (mixture - first - unit * second)
        emit(i, slice(0, D), part)

    def sums_of(l, g_ref):
        for n, ref in enumerate((gpre, gh, g_ref)):
            row = slice(4 * l + n, 4 * l + n + 1)
            vec[row, :] = col_sum(ref[...].astype(F32))
        vec[4 * l + 3 : 4 * l + 4, :] = jnp.zeros((1, D), F32)

    def weights_of(l, ch, g_ref):
        def rows_of(m, _):
            lanes = pl.ds(pl.multiple_of(m * 384, 128), 384)
            if ch == 0:
                value = dot_tn(nb[l, :, lanes], gh[...])
            elif ch == 1:
                value = dot_tn(g_ref[:, lanes], act[l])
            else:
                value = dot_tn(na[l, :, lanes], gpre[...])
                other = dot_tn(g_ref[:, lanes], mixp[l])
                value = jnp.concatenate(
                    [value[:, 0 : 2 * LOCAL], value[:, 2 * LOCAL :] + other], axis=1
                )
            grads[ch, pl.ds(4 * m, 4)] = value.astype(BF).reshape(4, 2, 48, D)
            return 0

        lax.fori_loop(0, 2, rows_of, 0)
        cp.start(("rc", l, ch), grads.at[ch, :, 1 - c], sib.at[l, ch], to_c)

    def weights_gone(l, ch):
        cp.sent_off(("rc", l, ch), grads.at[ch, :, 1 - c], sib.at[l, ch], to_c)

    def reduce_core(l, ch):
        cp.landed(("rc", l, ch), sib.at[l, ch])

        def add(i, _):
            sib[l, ch, i] = (sib[l, ch, i].astype(F32) + grads[ch, i, c].astype(F32)).astype(BF)
            return 0

        lax.fori_loop(0, 8, add, 0)
        for p in range(4):
            if REDUCE[p][0] == ch:
                reduce_start(l, p)

    def reduce_start(l, p):
        ch, lanes, x_first = REDUCE[p]
        if x_first:
            for j in (1, 3, 2, 0):
                yy = (y + j) % 4
                cp.start(
                    ("rx", l, p, j),
                    sib.at[l, ch, yy * 2 + 1 - x, :, lanes],
                    xbuf.at[l, ch - 1, yy, :, lanes],
                    to_x,
                )
        else:
            for j in (1, 3, 2):
                yy = (y + j) % 4
                cp.start(
                    ("ry", l, p, j),
                    sib.at[l, ch, pl.ds(yy * 2, 2), :, lanes],
                    ybuf.at[l, pl.ds(3 * ch + 2 * (j - 1), 2), :, lanes],
                    to_y[j],
                )

    def slot_of(p, j):
        return 11 + j if REDUCE[p][0] == 1 else 5 + j

    def reduce_mid(l, p):
        ch, lanes, x_first = REDUCE[p]
        if x_first:
            for j in (1, 3, 2, 0):
                yy = (y + j) % 4
                ref = xbuf.at[l, ch - 1, yy, :, lanes]
                cp.landed(("rx", l, p, j), ref)
                mine = sib[l, ch, yy * 2 + x, :, lanes].astype(F32)
                xbuf[l, ch - 1, yy, :, lanes] = (
                    mine + xbuf[l, ch - 1, yy, :, lanes].astype(F32)
                ).astype(BF)
                if j:
                    to = ybuf.at[l, slot_of(p, j), :, lanes]
                    cp.start(("ry", l, p, j), ref, to, to_y[j])
        else:
            for j in (1, 3, 2):
                cp.landed(
                    ("ry", l, p, j), ybuf.at[l, pl.ds(3 * ch + 2 * (j - 1), 2), :, lanes]
                )
            for i in range(2):
                total = sib[l, ch, y * 2 + i, :, lanes].astype(F32)
                for j in range(3):
                    total = total + ybuf[l, 3 * ch + 2 * j + i, :, lanes].astype(F32)
                keep[l, ch // 2, i, :, lanes] = total.astype(BF)
            cp.start(
                ("rx", l, p, 0),
                keep.at[l, ch // 2, 1 - x, :, lanes],
                keep.at[l, ch // 2, 2, :, lanes],
                to_x,
            )

    def sums_copy(l, p):
        ch, lanes, _ = REDUCE[p]
        return cp.make(("rs", p), sbuf.at[l, ch, :, lanes], sbuf_in.at[ch, :, lanes], to_s)

    def reduce_end(l, p):
        ch, lanes, x_first = REDUCE[p]
        if x_first:
            total = xbuf[l, ch - 1, y, :, lanes].astype(F32)
            for j in (1, 3, 2):
                cp.landed(("ry", l, p, j), ybuf.at[l, slot_of(p, j), :, lanes])
            for j in (1, 2, 3):
                total = total + ybuf[l, slot_of(p, j), :, lanes].astype(F32)
        else:
            cp.landed(("rx", l, p, 0), keep.at[l, ch // 2, 2, :, lanes])
            total = keep[l, ch // 2, x, :, lanes].astype(F32)
            total = total + keep[l, ch // 2, 2, :, lanes].astype(F32)
        sbuf[l, ch, :, lanes] = total.astype(BF)

        @pl.when(s == 1 - l)
        def _():
            sums_copy(l, p).start()

    def vec_z():
        vland[t, 0:8] = vec[8:16, :]
        for j in (1, 2, 3):
            cp.start(("vz", j), vec.at[pl.ds(8, 8)], vland.at[t, pl.ds(0, 8)], to_z[j])

    def vec_c():
        for j in (1, 2, 3):
            cp.landed(("vz", j), vland.at[(t + 4 - j) % 4, pl.ds(0, 8)])
        stage[0, 0:8] = vec[0:8, :]
        stage[0, 8:16] = vland[0, 0:8] + vland[1, 0:8] + vland[2, 0:8] + vland[3, 0:8]
        cp.start("vc", stage.at[0], vland.at[4], to_c)

    def vec_x():
        cp.landed("vc", vland.at[4])
        stage[1] = stage[0] + vland[4]
        cp.start("vx", stage.at[1], vland.at[5], to_x)

    def vec_s():
        cp.landed("vx", vland.at[5])
        stage[2] = stage[1] + vland[5]
        cp.start("vs", stage.at[2], vland.at[6], to_s)

    def vec_y():
        cp.landed("vs", vland.at[6])
        stage[3] = stage[2] + vland[6]
        vland[7 + y] = stage[3]
        for j in (1, 2, 3):
            cp.start(("vy", j), stage.at[3], vland.at[7 + y], to_y[j])

    swap_start(0)
    swap_wait(0, 2)
    gather_first(0, 0)
    gather_first(0, 1)
    prepare()
    gather_second(0, 0)
    gather_second(0, 1)
    swap_wait(0, 0)
    gather_first(0, 2)
    swap_wait(0, 1)
    gather_first(0, 3)
    swap_wait(0, None)
    swap_start(1)
    fetch_x.wait()
    norms(0, x0, 0)
    norms(0, x0, 1)
    gather_third(0, 0)
    gather_third(0, 1)
    norms(0, x0, 2)
    norms(0, x0, 3)
    gather_second(0, 2)
    gather_second(0, 3)
    gather_fourth(0, 0)
    gather_fourth(0, 1)
    gather_last(0, 0)
    gather_last(0, 1)
    project(0, 0, 256)
    project(0, 256, 256)
    attend(0, 0)
    gather_third(0, 2)
    gather_third(0, 3)
    swap_wait(1, 2)
    gather_first(1, 0)
    gather_first(1, 1)
    swap_wait(1, 0)
    gather_first(1, 2)
    swap_wait(1, 1)
    gather_first(1, 3)
    swap_wait(1, None)
    attend(0, 1)
    gather_fourth(0, 2)
    gather_fourth(0, 3)
    attend(0, 2)
    gather_second(1, 0)
    gather_second(1, 1)
    attend(0, 3)
    gather_second(1, 2)
    gather_second(1, 3)
    gather_last(0, 2)
    feed(0, 0)
    gather_last(0, 3)
    result_rows(0, 0, emit_row(0))
    row_push(0, 0)
    row_push(0, 1)
    gather_third(1, 0)
    gather_third(1, 1)
    feed(0, 1)
    result_rows(0, 1, emit_row(0))
    row_push(0, 2)
    row_push(0, 3)
    row_finish(0, 0, x0, 0, x1)
    row_finish(0, 1, x0, 0, x1)
    gather_third(1, 2)
    row_finish(0, 2, x0, 0, x1)
    gather_third(1, 3)
    row_finish(0, 3, x0, 0, x1)
    for p in range(4):
        gather_fourth(1, p)
    gather_last(1, 0)
    gather_last(1, 1)

    for i in range(2):
        row_wait(0, 2 * i, x1)
        norms(1, x1, 2 * i)
        row_wait(0, 2 * i + 1, x1)
        norms(1, x1, 2 * i + 1)
        project(1, 256 * i, 256)
        attend(1, 2 * i, 2 * i + 1)
        if i == 0:
            gather_last(1, 2)
        feed(1, i)
    gather_last(1, 3)

    fetch_g.wait()
    back_heads(1, g1, 1)
    back_heads(1, g1, 0)
    for i in (1, 0):
        back_attend(1, 2 * i + 1)
        back_attend(1, 2 * i)
        back_turn(2 * i + 1)
        back_turn(2 * i)
        back_norms(1, i, emit_row(1))
        row_push(1, 2 * i + 1)
        row_push(1, 2 * i)
    row_finish(1, 3, g1, None, g0)
    weights_of(1, 1, g1)
    row_finish(1, 2, g1, None, g0)
    weights_of(1, 0, g1)
    row_finish(1, 1, g1, None, g0)
    weights_of(1, 2, g1)
    row_finish(1, 0, g1, None, g0)
    reduce_core(1, 1)
    reduce_core(1, 0)
    sums_of(1, g1)
    reduce_core(1, 2)
    result_cols(1, 0)
    for i in range(4):
        col_push(0, i)
    pack(x1, acts.at[0, 0])
    for i in range(4):
        act_push(0, 0, i)
    for ch in range(3):
        weights_gone(1, ch)

    for i in (1, 0):
        row_wait(1, 2 * i + 1, g0)
        row_wait(1, 2 * i, g0)
        back_heads(0, g0, i)
        if i == 0:
            weights_of(0, 1, g0)
            weights_of(0, 0, g0)
            reduce_mid(1, 1)
            reduce_mid(1, 2)
            reduce_mid(1, 3)
            reduce_core(0, 1)
            pack(g0, acts.at[1, 1])
            for n in range(4):
                act_push(1, 1, n)
        back_attend(0, 2 * i + 1)
        if i == 1:
            reduce_mid(1, 0)
        else:
            reduce_core(0, 0)
        back_attend(0, 2 * i)
        if i == 1:
            for n in range(4):
                col_finish(0, n, acts.at[0, 0], 1, 1, 0)
        back_turn(2 * i + 1)
        back_turn(2 * i)
        back_norms(0, i, emit_full)
        turn_cols(1, i)
        col_push(1, 2 * i + 1)
        col_push(1, 2 * i)
    weights_of(0, 2, g0)
    for p in range(4):
        reduce_end(1, p)
    sums_of(0, g0)
    vec_z()
    reduce_core(0, 2)
    vec_c()
    reduce_mid(0, 0)
    reduce_mid(0, 1)
    vec_x()
    col_finish(1, 3, acts.at[1, 1], None, 0, 1)
    col_finish(1, 2, acts.at[1, 1], None, 0, 1)
    vec_s()
    reduce_mid(0, 3)
    reduce_end(0, 1)
    reduce_mid(0, 2)
    reduce_end(0, 0)
    col_finish(1, 1, acts.at[1, 1], None, 0, 1)
    col_finish(1, 0, acts.at[1, 1], None, 0, 1)
    vec_y()
    reduce_end(0, 3)
    reduce_end(0, 2)

    acts_out[0, s] = acts[s, 0]
    acts_out[1, s] = acts[s, 1]
    for kind in range(2):
        for i in range(4):
            cp.landed(("act", kind, i), acts_in.at[kind, :, part_of(i)])
        acts_out[kind, 1 - s] = acts_in[kind]
    for j in (1, 2, 3):
        cp.landed(("vy", j), vland.at[7 + (y + 4 - j) % 4])
    stage[4] = vland[7] + vland[8] + vland[9] + vland[10]
    vec_out[0:4] = jnp.where(s == 0, stage[4, 0:4], stage[4, 4:8])
    vec_out[4:8] = jnp.where(s == 0, stage[4, 8:12], stage[4, 12:16])
    for p, (ch, lanes, _) in enumerate(REDUCE):
        cp.landed(("rs", p), sbuf_in.at[ch, :, lanes])
        w_out[ch, :, lanes] = sbuf[s, ch, :, lanes].astype(F32) + sbuf_in[ch, :, lanes].astype(F32)
        cp.late(("rs", p), sums_copy(1 - s, p))
    for name, copy in swap(s):
        cp.late(name, copy)
    for kind in range(2):
        for i in range(4):
            cp.late(("act", kind, i), act_copy(1 - s, kind, i))
    cp.finish()


def mega(*arguments):
    dma = pltpu.SemaphoreType.DMA
    vmem = pl.BlockSpec(memory_space=pltpu.VMEM)
    smem = pl.BlockSpec(memory_space=pltpu.SMEM)
    anywhere = pl.BlockSpec(memory_space=pl.ANY)

    def bf(*shape):
        return pltpu.VMEM(shape, BF)

    def f32(*shape):
        return pltpu.VMEM(shape, F32)

    return pl.pallas_call(
        mega_kernel,
        out_shape=[
            jax.ShapeDtypeStruct((2, 2, LOCAL, SLOT), BF),
            jax.ShapeDtypeStruct((3, 48, D), F32),
            jax.ShapeDtypeStruct((8, D), F32),
        ],
        in_specs=[smem, vmem, anywhere, anywhere] + [vmem] * 9,
        out_specs=[vmem] * 3,
        scratch_shapes=[
            bf(2, 3, D, D),
            f32(2, 8, D),
            bf(SLOT, D),
            bf(SLOT, D),
            bf(SLOT, D),
            bf(SLOT, D),
            f32(3, SLOT, 128),
            f32(SLOT, SLOT),
            f32(2, SLOT, D),
            f32(2, SLOT, 128),
            bf(2, SLOT, D),
            bf(2, SLOT, D),
            bf(2, 3, SLOT, HD),
            bf(2, 3, SLOT, HD),
            bf(2, 3, SLOT, HD),
            f32(2, 3, 128, 1280),
            bf(2, SLOT, 2 * LOCAL),
            bf(2, SLOT, D),
            f32(2, SLOT, D),
            bf(3, SLOT, HD),
            bf(SLOT, D),
            f32(SLOT, 2 * LOCAL),
            f32(SLOT, LOCAL),
            bf(SLOT, D),
            bf(SLOT, D),
            bf(2, 4, 4, 32, D),
            bf(2, 4, LOCAL, SLOT),
            bf(2, 4, 3, 32, D),
            bf(2, 3, LOCAL, SLOT),
            bf(2, 2, LOCAL, SLOT),
            bf(2, LOCAL, SLOT),
            bf(3, 8, 2, 48, D),
            bf(2, 3, 8, 48, D),
            bf(2, 2, 4, 48, D),
            bf(2, 15, 48, D),
            bf(2, 2, 3, 48, D),
            bf(2, 3, 48, D),
            bf(3, 48, D),
            f32(16, D),
            f32(11, 16, D),
            f32(5, 16, D),
            dma((SEMS,)),
            dma((SEMS,)),
            dma((2,)),
        ],
        compiler_params=pltpu.CompilerParams(
            collective_id=0, has_side_effects=True, vmem_limit_bytes=VMEM_LIMIT
        ),
        name="two_layers",
    )(*arguments)


def hand_out_kernel(acts, sums, vec, sec, grad, wqkv, bqkv, wattn, win, bin_, wout, bout, gains, shifts):
    sec[...] = acts[0]
    grad[...] = acts[1]
    for n in range(3):
        lanes = slice(LOCAL * n, LOCAL * n + LOCAL)
        wqkv[n] = sums[2, :, lanes]
        bqkv[n] = vec[0:1, lanes]
    wattn[...] = sums[2, :, 3 * LOCAL :]
    win[...] = sums[0]
    wout[...] = sums[1]
    bin_[...] = vec[1:2, :]
    bout[...] = vec[2:3, :]
    gains[...] = vec[4:6, :]
    shifts[...] = vec[6:8, :]


def hand_out(acts, sums, vec):
    vmem = pl.BlockSpec(memory_space=pltpu.VMEM)
    shapes = [(3, 48, LOCAL), (3, 1, LOCAL), (48, LOCAL), (48, D), (1, D), (48, D), (1, D)]
    return pl.pallas_call(
        hand_out_kernel,
        out_shape=[jax.ShapeDtypeStruct((2, LOCAL, SLOT), BF)] * 2
        + [jax.ShapeDtypeStruct(shape, F32) for shape in shapes + [(2, D), (2, D)]],
        in_specs=[vmem] * 3,
        out_specs=[vmem] * 11,
        name="hand_out",
    )(acts, sums, vec)


def body(
    inputs,
    cotangent,
    seq_lengths,
    w_qkv,
    b_qkv,
    w_attn_out,
    w_in,
    b_in,
    w_out,
    b_out,
    norm_gains,
    norm_biases,
):
    powers = 1.0 / 10000.0 ** (np.arange(ROT // 2, dtype=np.float32) * 2.0 / ROT)
    freq = jnp.asarray(np.tile(powers.astype(np.float32), 128 // (ROT // 2))[None])
    acts, sums, vec = mega(
        seq_lengths[:, 0],
        freq,
        inputs,
        cotangent,
        w_qkv[0].transpose(1, 0, 2),
        w_attn_out[0].T,
        w_in[0],
        w_out[0].T,
        b_qkv.transpose(1, 0, 2),
        b_in,
        b_out,
        norm_gains[0],
        norm_biases[0],
    )
    sec, grad, wqkv, bqkv, wattn, win, bin_, wout, bout, gains, shifts = hand_out(acts, sums, vec)
    return (
        sec.transpose(0, 2, 1)[None],
        grad.transpose(0, 2, 1)[None],
        wqkv.transpose(1, 0, 2)[None],
        bqkv.transpose(1, 0, 2),
        wattn.T[None],
        win[None],
        bin_,
        wout.T[None],
        bout,
        gains[None],
        shifts[None],
    )


def solution(mesh):
    return jax.shard_map(
        body,
        mesh=mesh,
        in_specs=(
            P(None, "dp", None),
            P(None, "dp", None),
            P(None, "dp", None),
            P("section", "dp", None, "tensor"),
            P("section", None, "tensor"),
            P("section", "tensor", "dp"),
            P("section", "dp", "tensor"),
            P("section", "tensor"),
            P("section", "tensor", "dp"),
            P("section", None),
            P("section", None, None),
            P("section", None, None),
        ),
        out_specs=(
            P("section", None, "dp", "tensor"),
            P("section", None, "dp", "tensor"),
            P("section", "dp", None, "tensor"),
            P("section", None, "tensor"),
            P("section", "tensor", "dp"),
            P("section", "dp", "tensor"),
            P("section", "tensor"),
            P("section", "tensor", "dp"),
            P("section", None),
            P("section", None, None),
            P("section", None, None),
        ),
        check_vma=False,
    )
```
